128 devices in a mesh: stream: 8 (over x, core), depth: 16 (over y, z).
Axes of the slice: x: 4, y: 4, z: 4, core: 2. Of those that a mesh axis runs over, the one named last changes fastest.
Arguments:
- velocity: bfloat16 [3, 512, 768, 128], P(None, 'stream', 'depth'), may hold values from -6 to 6
- diffusion: bfloat16 [512, 768, 128], P('stream', 'depth'), may hold values from 0.0099487305 to 0.05493164
- advection: bfloat16 [512, 768, 128], P('stream', 'depth'), may hold values from 0.049804688 to 0.29882812
- normals: bfloat16 [8, 16, 3, 128, 128], P('stream', 'depth'), may hold values from -3 to 3
- tile_cell: int32 [8, 16, 128], P('stream', 'depth'), may hold values from 0 to 3071
- tile_class: int32 [8, 16, 128], P('stream', 'depth'), may hold values from 0 to 7
- tile_leaf: int32 [8, 16, 128], P('stream', 'depth'), may hold values from 0 to 63
- tile_owner: int32 [8, 16, 128, 1], P('stream', 'depth'), may hold values from 0 to 127; in each aligned block of 128 rows (0 to 127, 128 to 255, ..., all dimensions but the last counted through in order) at most 2 rows name the same one
- source_expansion: bfloat16 [8, 128, 289], replicated, may hold values from -0.5 to 0.5
- translation: float32 [8, 289, 289], replicated, may hold values from -0.125 to 0.125
- leaf_octant: int32 [8, 16, 8, 8], P('stream', 'depth'), may hold values from 0 to 7, each once within a row
- node_octant: int32 [8, 16, 8], P('stream', 'depth'), may hold values from 0 to 7, each once within a row
- subtree_octant: int32 [8, 2, 8], P('stream'), may hold values from 0 to 7, each once within a row
- cluster_octant: int32 [2, 8], replicated, may hold values from 0 to 7, each once within a row
- root_octant: int32 [8], replicated, may hold values from 0 to 7, each once
Outputs:
- flow: float32 [3, 512, 768, 128], P(None, 'stream', 'depth')
- leaf_multipoles: float32 [8, 16, 64, 289], P('stream', 'depth')
- upper_multipoles: float32 [19, 289], replicated
The draws below stay inside these ranges and needn't reach their ends.
Inputs may be any that keep to these rules, and one draw needn't show every extreme that they name: `tile_owner`: among the tiles of one device no owner is named more than 2 times, a bound that some block reaches. Owners are numbered with the stream index slowest. `tile_cell`: cells of a device's block are numbered with the depth index fastest. `leaf_octant`: each row of eight holds every octant once. `node_octant`: each row of eight holds every octant once. `subtree_octant`: each row of eight holds every octant once. `cluster_octant`: each row of eight holds every octant once. `root_octant`: holds every octant once.
All inputs are finite; a program needn't handle non-finite values.
Results may differ from the reference program's by a relative error of at most 0.0029.
Values may be sent and summed in bfloat16 or wider, within the bound.
A program may use at most 192 MiB of HBM per device.

```python
import math
import jax
import jax.numpy as jnp
import numpy as np
from jax import lax

SX = 64
SD = 48
SPAN = 128
SWEEPS = 4
TILE_DEV = 128
COEF = 289
LEAF_DEV = 64
CAP = 2
GROUPS = 2
NX = 512
ND = 768
N_STREAM = 8
N_DEPTH = 16
DEVICES = 128


def place_ends(array, rng, low, top_value):
    extent = array.shape
    place = [jax.random.randint(jax.random.fold_in(rng, axis), (), 0, extent[axis]) for axis in range(len(extent))]
    array = array.at[tuple(place)].set(low)
    longest = extent.index(max(extent))
    place[longest] = (place[longest] + 1) % extent[longest]
    return array.at[tuple(place)].set(top_value)


def block_scale(rng, shape, pieces, low, top_value):
    gain, own = 1.0, jax.random.fold_in(rng, 6)
    for axis_at, blocks in pieces:
        draws = jnp.exp(jax.random.uniform(jax.random.fold_in(own, axis_at), (blocks,), jnp.float32, low / len(pieces), top_value / len(pieces)))
        gain = gain * jnp.repeat(draws, shape[axis_at] // blocks).reshape([-1 if axis == axis_at else 1 for axis in range(len(shape))])
    return gain


def shared_out(own_key, own, number, rows, count, top, most, slope):
    ranking = jax.random.permutation(own_key, count)
    crowded, ordinary = load_shares(count, rows * top, most, slope, True), load_shares(count, rows * top, most, slope, False)
    places = jnp.arange(count)

    def named(tallies, offset_by):
        used = int((tallies > 0).sum())
        fixed = max(1, used // 4)
        shifted = fixed + (places - fixed + offset_by * (used - fixed)) % max(1, count - fixed)
        return jnp.zeros((count,), jnp.int32).at[ranking[jnp.where(places < fixed, places, shifted)]].set(jnp.asarray(tallies, jnp.int32))

    tallies = jnp.where(number % 4 == 0, named(crowded, number // 4), named(ordinary, number - number // 4 - 1))
    mixed = jax.random.permutation(jax.random.fold_in(own, 3), count)
    donor, taker = mixed[0:count // 2 * 2:2], mixed[1:count // 2 * 2:2]
    slack = jnp.minimum(tallies[donor] - 1, most - tallies[taker]) // 2
    slack = jnp.where((donor == ranking[0]) | (taker == ranking[0]) | (tallies[taker] == 0), 0, jnp.maximum(slack, 0))
    shifted = jax.random.randint(jax.random.fold_in(own, 4), (count // 2,), 0, 1 << 20) % (slack + 1)
    tallies = tallies.at[donor].add(-shifted).at[taker].add(shifted)
    items = jnp.searchsorted(jnp.cumsum(tallies), jnp.arange(rows * top), side="right").astype(jnp.int32)
    listing = items.reshape(top, rows).T
    listing = listing[jax.random.permutation(jax.random.fold_in(own, 1), rows)]
    offset_by = jax.random.randint(jax.random.fold_in(own, 2), (rows, 1), 0, top)
    return jnp.take_along_axis(listing, (jnp.arange(top)[None, :] + offset_by) % top, axis=1)


def load_shares(amount, total, most, lean, full):
    weights = [(1 << 20) // math.isqrt(rank ** lean) + 1 for rank in range(1, amount + 1)]
    largest = most if full else min(most, max(-(-total // amount), total * weights[0] // sum(weights)))
    least = 1 if total - largest >= amount - 1 else 0
    given, spare = [largest] + [least] * (amount - 1), total - largest - least * (amount - 1)
    while spare > 0:
        movable = [i for i in range(1, amount) if given[i] < largest] or [i for i in range(1, amount) if given[i] < most]
        pool, left = sum([weights[i] for i in movable]), spare
        for i in movable:
            more = min(most - given[i], max(1, left * weights[i] // pool), spare)
            given[i] = given[i] + more
            spare = spare - more
    return np.array(given)


def centred(rng, dims, width, bound, split=(), held_as=jnp.bfloat16):
    loudness = block_scale(rng, dims, split, -0.22, 0.18) if split else 1.0
    values = jax.random.normal(rng, dims, jnp.float32) * width * loudness
    return jnp.minimum(jnp.maximum(values, -bound), bound).astype(held_as)


def setup_inputs(seed: int = 0) -> dict:
    seeds = jax.random.split(jax.random.key(seed), 16)
    velocity = centred(seeds[0], (3, NX, ND, SPAN), 1.0, 6.0, ((1, 8), (2, 16)))
    diffusion = jnp.clip(jnp.exp(math.log(0.05493164) - 1.70864456 * jax.random.uniform(seeds[1], (NX, ND, SPAN), jnp.float32) ** block_scale(seeds[1], (NX, ND, SPAN), ((0, 8), (1, 16)), -0.2, 0.2)), 0.0099487305, 0.05493164).astype(jnp.bfloat16)
    advection = jnp.clip(jnp.exp(math.log(0.29882812) - 1.7917595 * jax.random.uniform(seeds[2], (NX, ND, SPAN), jnp.float32) ** block_scale(seeds[2], (NX, ND, SPAN), ((0, 8), (1, 16)), -0.2, 0.2)), 0.049804688, 0.29882812).astype(jnp.bfloat16)
    normals = centred(seeds[3], (N_STREAM, N_DEPTH, 3, TILE_DEV, SPAN), 0.577, 3.0, ((0, 8), (1, 16)))
    tile_cell = place_ends(jax.random.randint(seeds[4], (N_STREAM, N_DEPTH, TILE_DEV), 0, SX * SD), jax.random.fold_in(seeds[4], 1), 0, (SX * SD) - 1).astype(jnp.int32)
    tile_class = place_ends(jax.random.randint(seeds[5], (N_STREAM, N_DEPTH, TILE_DEV), 0, 8), jax.random.fold_in(seeds[5], 1), 0, 7).astype(jnp.int32)
    tile_leaf = place_ends(jax.random.randint(seeds[6], (N_STREAM, N_DEPTH, TILE_DEV), 0, LEAF_DEV), jax.random.fold_in(seeds[6], 1), 0, LEAF_DEV - 1).astype(jnp.int32)
    tile_owner_keys = jax.random.split(jax.random.fold_in(seeds[7], 1), N_STREAM * N_DEPTH * TILE_DEV // TILE_DEV)
    tile_owner_turns = jax.random.permutation(jax.random.fold_in(seeds[7], 3), N_STREAM * N_DEPTH * TILE_DEV // TILE_DEV)
    tile_owner = jax.vmap(lambda own, number: shared_out(jax.random.fold_in(seeds[7], 2), own, number, TILE_DEV, DEVICES, 1, CAP, 2))(tile_owner_keys, tile_owner_turns).reshape((N_STREAM, N_DEPTH, TILE_DEV, 1))
    source_expansion = centred(seeds[8], (8, SPAN, COEF), SPAN ** -0.5, 0.5)
    translation = centred(seeds[9], (8, COEF, COEF), (8 * COEF) ** -0.5, 0.125, (), jnp.float32)
    leaf_octant = jax.vmap(lambda own: jax.random.permutation(own, 8))(jax.random.split(seeds[10], N_STREAM * N_DEPTH * 8)).reshape((N_STREAM, N_DEPTH, 8, 8)).astype(jnp.int32)
    node_octant = jax.vmap(lambda own: jax.random.permutation(own, 8))(jax.random.split(seeds[11], N_STREAM * N_DEPTH)).reshape((N_STREAM, N_DEPTH, 8)).astype(jnp.int32)
    subtree_octant = jax.vmap(lambda own: jax.random.permutation(own, 8))(jax.random.split(seeds[12], N_STREAM * GROUPS)).reshape((N_STREAM, GROUPS, 8)).astype(jnp.int32)
    cluster_octant = jax.vmap(lambda own: jax.random.permutation(own, 8))(jax.random.split(seeds[13], GROUPS)).reshape((GROUPS, 8)).astype(jnp.int32)
    root_octant = jax.random.permutation(seeds[14], 8).astype(jnp.int32)
    return dict(velocity=velocity, diffusion=diffusion, advection=advection, normals=normals, tile_cell=tile_cell, tile_class=tile_class, tile_leaf=tile_leaf, tile_owner=tile_owner, source_expansion=source_expansion, translation=translation, leaf_octant=leaf_octant, node_octant=node_octant, subtree_octant=subtree_octant, cluster_octant=cluster_octant, root_octant=root_octant)


def translate(children, octants, table):
    select = (octants[..., None] == jnp.arange(8, dtype=jnp.int32)).astype(jnp.float32)
    grouped = jnp.einsum("...ko,...kc->...oc", select, children, precision=lax.Precision.HIGHEST)
    return jnp.einsum("...oc,ocd->...d", grouped, table, precision=lax.Precision.HIGHEST)


def expand(strength, classes, table):
    count = strength.shape[0]
    pick = (classes[:, None] == jnp.arange(8, dtype=jnp.int32)).astype(strength.dtype)
    stacked = (pick[:, :, None] * strength[:, None, :]).reshape(count, 8 * strength.shape[1])
    return jnp.dot(stacked, table.reshape(8 * table.shape[1], table.shape[2]), preferred_element_type=jnp.float32)


def advance(padded, centre, kappa, speed):
    forward = padded[:, 2:, 1:-1]
    backward = padded[:, :-2, 1:-1]
    above_cell = padded[:, 1:-1, 2:]
    below_cell = padded[:, 1:-1, :-2]
    spanwise = jnp.roll(centre, 1, axis=3) + jnp.roll(centre, -1, axis=3)
    total = forward + backward + above_cell + below_cell + spanwise - 6.0 * centre
    return centre + kappa * total - speed * (centre - backward)


def reference(velocity, diffusion, advection, normals, tile_cell, tile_class, tile_leaf, tile_owner, source_expansion, translation, leaf_octant, node_octant, subtree_octant, cluster_octant, root_octant):
    field = velocity.astype(jnp.float32)
    kappa = diffusion.astype(jnp.float32)
    speed = advection.astype(jnp.float32)
    for sweep in range(SWEEPS):
        padded = jnp.pad(field, ((0, 0), (1, 1), (1, 1), (0, 0)))
        field = advance(padded, field, kappa, speed)
    rows = jnp.arange(N_STREAM, dtype=jnp.int32)[:, None, None] * SX + tile_cell // SD
    cols = jnp.arange(N_DEPTH, dtype=jnp.int32)[None, :, None] * SD + tile_cell % SD
    picked = jnp.moveaxis(field[:, rows, cols, :], 0, 2)
    strength = jnp.sum(normals.astype(jnp.float32) * picked, axis=2).astype(jnp.bfloat16)
    tiles = N_STREAM * N_DEPTH * TILE_DEV
    terms = expand(strength.reshape(tiles, SPAN), tile_class.reshape(tiles), source_expansion)
    target = tile_owner.reshape(tiles) * LEAF_DEV + tile_leaf.reshape(tiles)
    leaves = jax.ops.segment_sum(terms, target, num_segments=N_STREAM * N_DEPTH * LEAF_DEV)
    leaves = leaves.reshape(N_STREAM, N_DEPTH, LEAF_DEV, COEF)
    level4 = translate(leaves.reshape(N_STREAM, N_DEPTH, 8, 8, COEF), leaf_octant, translation)
    subtree = translate(level4, node_octant, translation)
    cluster = translate(subtree.reshape(N_STREAM, GROUPS, 8, COEF), subtree_octant, translation)
    half = translate(jnp.transpose(cluster, (1, 0, 2)), cluster_octant[:, :N_STREAM], translation)
    root = translate(half[None], root_octant[None, :GROUPS], translation)
    upper = jnp.concatenate([cluster.reshape(N_STREAM * GROUPS, COEF), half, root], axis=0)
    return field, leaves, upper
```

```python
import functools

import jax
import jax.numpy as jnp
from jax import lax
from jax.experimental import pallas as pl
from jax.experimental.pallas import tpu as pltpu
from jax.sharding import PartitionSpec as P

MESH = pl.DeviceIdType.MESH
F32, BF16, I32 = jnp.float32, jnp.bfloat16, jnp.int32
SX, SD, SPAN, SWEEPS, TILES, COEF, LEAVES = 64, 48, 128, 4, 128, 289, 64
NS, ND = 8, 16
SLAB, LEAD = 64, 8
KP = 384
KR = 304
SLOTS = 2 * NS * ND


def split(value):
    high = value.astype(BF16).astype(F32)
    return high, value - high


def dot(a, b):
    return jnp.dot(a, b, preferred_element_type=F32)


def dot_nt(a, b):
    return lax.dot_general(a, b, (((1,), (1,)), ((), ())), preferred_element_type=F32)


def iota(shape, dim):
    return lax.broadcasted_iota(I32, shape, dim)


def kernel(
    cell, loct, noct, soct, coct, roct,
    owner, cls, leaf,
    vel, dif, adv, nrm, exp, tr,
    flow, leaves, upper,
    velv, difv, advv, nrmv, expv, trv, tv, ef, et, wh, wl, qa, qb, al, ka, be,
    pmat, perm, gg, picked, order,
    xs, xr, ds, dr, m1s, m1r, m2s, m2r, a1s, a1r, a2s, a2r, e1s, e1r, e2s, e2r,
    lsem, hss, hrs, m1ss, m1rs, m2ss, m2rs, a1ss, a1rs, a2ss, a2rs, e1ss, e1rs, e2ss, e2rs,
):
    i, j = lax.axis_index("stream"), lax.axis_index("depth")

    loads = [
        pltpu.make_async_copy(s, d, lsem.at[n])
        for n, (s, d) in enumerate(
            (
                (vel, velv),
                (dif, difv),
                (adv, advv),
                (nrm, nrmv),
                (exp, expv),
                (tr.at[:, pl.ds(0, SPAN)], tv.at[0, pl.ds(0, 8 * COEF), :]),
                (tr.at[:, pl.ds(SPAN, SPAN)], tv.at[1, pl.ds(0, 8 * COEF), :]),
                (tr.at[:, pl.ds(2 * SPAN, COEF - 2 * SPAN)], trv),
            )
        )
    ]
    for copy in loads:
        copy.start()

    barrier = pltpu.get_barrier_semaphore()
    for r in range(1, ND):
        pl.semaphore_signal(barrier, inc=1, device_id=(i, lax.rem(j + r, ND)), device_id_type=MESH)
    for r in range(1, NS):
        pl.semaphore_signal(barrier, inc=1, device_id=(lax.rem(i + r, NS), j), device_id_type=MESH)

    def along_depth(src, dst, ss, rs):
        return [
            pltpu.make_async_remote_copy(
                src_ref=src(lax.rem(j + r, ND)), dst_ref=dst.at[j], send_sem=ss.at[r], recv_sem=rs.at[r],
                device_id=(i, lax.rem(j + r, ND)), device_id_type=MESH,
            )
            for r in range(1, ND)
        ]

    def along_stream(src, dst, ss, rs):
        return [
            pltpu.make_async_remote_copy(
                src_ref=src(lax.rem(i + r, NS)), dst_ref=dst.at[i], send_sem=ss.at[r], recv_sem=rs.at[r],
                device_id=(lax.rem(i + r, NS), j), device_id_type=MESH,
            )
            for r in range(1, NS)
        ]

    def start(copies):
        for copy in copies:
            copy.start()

    def arrive(copies):
        for copy in copies:
            copy.wait_recv()

    def sent(copies):
        for copy in copies:
            copy.wait_send()

    def halo(n):
        xlow = velv.at[:, 0] if n == 0 else xs.at[n, 0]
        xhigh = velv.at[:, SX - 1] if n == 0 else xs.at[n, 1]

        def copy(src, dst, which, device):
            return pltpu.make_async_remote_copy(
                src_ref=src, dst_ref=dst, send_sem=hss.at[n, which], recv_sem=hrs.at[n, which],
                device_id=device, device_id_type=MESH,
            )

        return (
            (i < NS - 1, i > 0, copy(xhigh, xr.at[n, 0], 0, (lax.rem(i + 1, NS), j))),
            (i > 0, i < NS - 1, copy(xlow, xr.at[n, 1], 1, (lax.rem(i + NS - 1, NS), j))),
            (j < ND - 1, j > 0, copy(ds.at[n, 1], dr.at[n, 0], 2, (i, lax.rem(j + 1, ND)))),
            (j > 0, j < ND - 1, copy(ds.at[n, 0], dr.at[n, 1], 3, (i, lax.rem(j + ND - 1, ND)))),
        )

    def halo_start(n):
        for send, _, copy in halo(n):
            pl.when(send)(copy.start)

    def halo_arrive(n):
        for _, receive, copy in halo(n):
            pl.when(receive)(copy.wait_recv)

    def halo_sent(n):
        for send, _, copy in halo(n):
            pl.when(send)(copy.wait_send)

    for edge, ref, side in ((i == 0, xr, 0), (i == NS - 1, xr, 1), (j == 0, dr, 0), (j == ND - 1, dr, 1)):

        @pl.when(edge)
        def _(ref=ref, side=side):
            for n in range(SWEEPS):
                ref[n, side] = jnp.zeros(ref.shape[2:], BF16)

    zero8 = jnp.zeros((8, SPAN), F32)
    for q in (qa, qb):
        for k in range(3):
            for x in (0, SX + 1):
                q[k, pl.ds(x * SLAB, SLAB), :] = jnp.zeros((SLAB, SPAN), F32)

    def clear(x, carry):
        for q in (qa, qb):
            for k in range(3):
                q[k, pl.ds(pl.multiple_of(x * SLAB, 8), 8), :] = zero8
                q[k, pl.ds(pl.multiple_of(x * SLAB + LEAD + SD, 8), 8), :] = zero8
        return carry

    lax.fori_loop(1, SX + 1, clear, 0)

    own = owner[...]
    across = jnp.broadcast_to(own.astype(F32), (TILES, TILES))
    down = jnp.transpose(across)
    before = iota((TILES, TILES), 0) < iota((TILES, TILES), 1)
    rank = jnp.sum(jnp.where((across == down) & before, 1.0, 0.0), axis=0, keepdims=True).astype(I32)
    slot = (own & (ND - 1)) * (2 * NS) + (own >> 4) * 2 + rank
    pmat[...] = jnp.where(iota((SLOTS, TILES), 0) == slot, 1.0, 0.0).astype(BF16)
    feature = iota((SPAN, TILES), 0)
    meta = jnp.where((feature == leaf[...]) | (feature == cls[...] + LEAVES), 1.0, 0.0).astype(BF16)
    m1s[...] = dot_nt(pmat[...], meta).astype(BF16).reshape(ND, 2 * NS, SPAN)
    out = iota((SLOTS, SLOTS), 0)
    source = ((out >> 1) & (ND - 1)) * (2 * NS) + (out >> 5) * 2 + (out & 1)
    perm[...] = jnp.where(iota((SLOTS, SLOTS), 1) == source, 1.0, 0.0).astype(BF16)

    for copy in loads[:3]:
        copy.wait()

    def widen(x, carry):
        at = pl.multiple_of((x + 1) * SLAB + LEAD, 8)
        for k in range(3):
            qa[k, pl.ds(at, SD), :] = velv[k, x].astype(F32)
        kappa = difv[x].astype(F32)
        speed = advv[x].astype(F32)
        rows = pl.ds(pl.multiple_of(x * SD, 8), SD)
        ka[rows, :] = kappa
        be[rows, :] = kappa + speed
        al[rows, :] = 1.0 - 6.0 * kappa - speed
        return carry

    lax.fori_loop(0, SX, widen, 0)
    low = pl.ds(SLAB + LEAD, SX, stride=SLAB)
    high = pl.ds(SLAB + LEAD + SD - 1, SX, stride=SLAB)
    for k in range(3):
        ds[0, 0, k] = qa[k, low, :].astype(BF16)
        ds[0, 1, k] = qa[k, high, :].astype(BF16)

    pl.semaphore_wait(barrier, ND - 1 + NS - 1)
    halo_start(0)
    meta1 = along_depth(lambda p: m1s.at[p], m1r, m1ss, m1rs)
    start(meta1)
    m1r[j] = m1s[j]

    def sweep(src, dst, pitch, lead):
        def step(x, carry):
            rows = pl.ds(pl.multiple_of(x * SD, 8), SD)
            kappa, beta, alpha = ka[rows, :], be[rows, :], al[rows, :]
            at = (x + 1) * SLAB + LEAD
            for k in range(3):
                view = src.at[k]
                c = view[pl.ds(pl.multiple_of(at, 8), SD), :]
                f = view[pl.ds(pl.multiple_of(at + SLAB, 8), SD), :]
                b = view[pl.ds(pl.multiple_of(at - SLAB, 8), SD), :]
                up = view[pl.ds(at + 1, SD), :]
                down = view[pl.ds(at - 1, SD), :]
                total = f + (up + down) + (pltpu.roll(c, 1, 1) + pltpu.roll(c, SPAN - 1, 1))
                dst[k, pl.ds(pl.multiple_of(x * pitch + lead, 8), SD), :] = alpha * c + kappa * total + beta * b
            return carry

        lax.fori_loop(0, SX, step, 0)

    def faces(n, dst, pitch, lead):
        first = pl.ds(lead, SD)
        last = pl.ds((SX - 1) * pitch + lead, SD)
        low = pl.ds(lead, SX, stride=pitch)
        high = pl.ds(lead + SD - 1, SX, stride=pitch)
        klow = ka[pl.ds(0, SX, stride=SD), :]
        khigh = ka[pl.ds(SD - 1, SX, stride=SD), :]
        for k in range(3):
            dst[k, first, :] = dst[k, first, :] + be[pl.ds(0, SD), :] * xr[n, 0, k].astype(F32)
            dst[k, last, :] = dst[k, last, :] + ka[pl.ds((SX - 1) * SD, SD), :] * xr[n, 1, k].astype(F32)
            ql = dst[k, low, :] + klow * dr[n, 0, k].astype(F32)
            qh = dst[k, high, :] + khigh * dr[n, 1, k].astype(F32)
            dst[k, low, :] = ql
            dst[k, high, :] = qh
            if n + 1 < SWEEPS:
                ds[n + 1, 0, k] = ql.astype(BF16)
                ds[n + 1, 1, k] = qh.astype(BF16)
                xs[n + 1, 0, k] = dst[k, first, :].astype(BF16)
                xs[n + 1, 1, k] = dst[k, last, :].astype(BF16)
        if n + 1 < SWEEPS:
            halo_start(n + 1)

    sweep(qa, qb, SLAB, SLAB + LEAD)
    for copy in loads[5:]:
        copy.wait()
    for w in (wh, wl):
        for o in range(8):
            w[o, pl.ds(KR, KP - KR), :] = jnp.zeros((KP - KR, KP), BF16)
    tv[:, pl.ds(8 * COEF, 8 * (KR - COEF)), :] = jnp.zeros((3, 8 * (KR - COEF), SPAN), F32)
    tv[2, pl.ds(0, 8 * COEF), :] = jnp.concatenate(
        [trv[...], jnp.zeros((8 * COEF, KP - COEF), F32)], axis=1
    )

    def halve(b, carry):
        for o in range(8):
            rows = pl.ds(b * 128 + o, 16, stride=8)
            to = pl.ds(pl.multiple_of(b * 16, 16), 16)
            for n in range(3):
                lanes = pl.ds(n * SPAN, SPAN)
                h, l = split(tv[n, rows, :])
                wh[o, to, lanes] = h.astype(BF16)
                wl[o, to, lanes] = l.astype(BF16)
        return carry

    lax.fori_loop(0, KR // 16, halve, 0)
    halo_arrive(0)
    faces(0, qb, SLAB, SLAB + LEAD)

    sweep(qb, qa, SLAB, SLAB + LEAD)
    arrive(meta1)
    m2s[...] = dot(perm[...], m1r[...].reshape(SLOTS, SPAN)).astype(BF16).reshape(NS, 2 * ND, SPAN)
    meta2 = along_stream(lambda p: m2s.at[p], m2r, m2ss, m2rs)
    start(meta2)
    m2r[i] = m2s[i]
    loads[4].wait()
    et[pl.ds(KR, KP - KR), :] = jnp.zeros((KP - KR, 8 * SPAN), BF16)
    ef[pl.ds(0, 8 * COEF), :] = expv[...].astype(F32)
    ef[pl.ds(8 * COEF, 8 * (KR - COEF)), :] = jnp.zeros((8 * (KR - COEF), SPAN), F32)

    def classes(b, carry):
        for c in range(8):
            value = ef[pl.ds(b * 128 + c, 16, stride=8), :]
            et[pl.ds(pl.multiple_of(b * 16, 16), 16), pl.ds(c * SPAN, SPAN)] = value.astype(BF16)
        return carry

    lax.fori_loop(0, KR // 16, classes, 0)
    halo_arrive(1)
    faces(1, qa, SLAB, SLAB + LEAD)

    sweep(qa, qb, SLAB, SLAB + LEAD)
    arrive(meta2)
    lane = iota((1, SPAN), 1)
    octant = jnp.full((1, SPAN), -1, I32)
    for l in range(LEAVES):
        octant = jnp.where(lane == l, loct[l // 8, l % 8], octant)
    row = iota((SPAN, SPAN), 0)
    ordered = jnp.where((row & 7) == (lane >> 3), jnp.where((row >> 3) == octant, 1.0, 0.0), 0.0)
    order[...] = jnp.transpose(ordered).astype(BF16)
    arrived = m2r[...].reshape(SLOTS, SPAN)
    leaf_of = dot_nt(ordered[:LEAVES].astype(BF16), arrived)
    pick = jnp.where(iota((8, SPAN), 1) == iota((8, SPAN), 0) + LEAVES, 1.0, 0.0).astype(BF16)
    class_of = dot_nt(pick, arrived)
    for c in range(8):
        gg[pl.ds(c * LEAVES, LEAVES), :] = (leaf_of * class_of[c : c + 1, :]).astype(BF16)
    halo_arrive(2)
    faces(2, qb, SLAB, SLAB + LEAD)

    sweep(qb, flow, SD, 0)
    halo_arrive(3)
    faces(3, flow, SD, 0)

    loads[3].wait()

    def sample(t, carry):
        for k in range(3):
            picked[k, t] = flow[k, cell[0, t]]
        return carry

    lax.fori_loop(0, TILES, sample, 0, unroll=8)
    strength = nrmv[0].astype(F32) * picked[0]
    for k in (1, 2):
        strength = strength + nrmv[k].astype(F32) * picked[k]
    a1s[...] = dot(pmat[...], strength.astype(BF16)).astype(BF16).reshape(ND, 2 * NS, SPAN)
    data1 = along_depth(lambda p: a1s.at[p], a1r, a1ss, a1rs)
    start(data1)
    a1r[j] = a1s[j]
    arrive(data1)
    a2s[...] = dot(perm[...], a1r[...].reshape(SLOTS, SPAN)).astype(BF16).reshape(NS, 2 * ND, SPAN)
    data2 = along_stream(lambda p: a2s.at[p], a2r, a2ss, a2rs)
    start(data2)
    a2r[i] = a2s[i]
    arrive(data2)

    sums = dot(gg[...], a2r[...].reshape(SLOTS, SPAN))
    blocks = []
    for c in range(8):
        h, l = split(sums[c * LEAVES : (c + 1) * LEAVES])
        blocks.append(jnp.concatenate([h, l], axis=0).astype(BF16))
    both = dot_nt(jnp.concatenate(blocks, axis=1), et[...])
    ordered_leaves = both[:LEAVES] + both[LEAVES:]

    h, l = split(ordered_leaves)
    lhs = jnp.concatenate(
        [jnp.concatenate([h[8 * o : 8 * o + 8], l[8 * o : 8 * o + 8]], axis=0).astype(BF16) for o in range(8)], axis=1
    )
    product = dot(lhs, wh[...].reshape(8 * KP, KP)) + dot(lhs, wl[...].reshape(8 * KP, KP))
    h, l = split(product[:8] + product[8:])
    node = iota((16, KP), 0) & 7
    octant = jnp.full((16, KP), -1, I32)
    for p in range(8):
        octant = jnp.where(node == p, noct[0, p], octant)
    stacked = jnp.concatenate([h, l], axis=0)
    lhs = jnp.concatenate([jnp.where(octant == o, stacked, 0.0).astype(BF16) for o in range(8)], axis=1)
    subtree = jnp.sum(dot(lhs, wh[...].reshape(8 * KP, KP)) + dot(lhs, wl[...].reshape(8 * KP, KP)), axis=0, keepdims=True)

    group, member = j >> 3, j & 7

    def lift(vector, which):
        h, l = split(vector)
        place = iota((16, KP), 0)
        rows = jnp.where(place == 0, h, jnp.where(place == 1, l, 0.0)).astype(BF16)
        return jnp.sum(dot(rows, wh[which]) + dot(rows, wl[which]), axis=0, keepdims=True)

    in_cluster = lift(subtree, soct[group, member])
    in_half = lift(in_cluster, coct[group, i])
    in_root = lift(in_half, roct[0, group])
    e1s[...] = jnp.concatenate([in_cluster, in_half, in_root], axis=1)
    terms = along_depth(lambda p: e1s, e1r, e1ss, e1rs)
    start(terms)
    e1r[j] = e1s[...]

    h, rest = split(ordered_leaves)
    m, l = split(rest)
    turn = order[:LEAVES, :LEAVES]
    leaves[...] = (dot(turn, h.astype(BF16)) + dot(turn, m.astype(BF16)) + dot(turn, l.astype(BF16)))[:, :COEF]

    arrive(terms)
    halves = []
    for g in range(2):
        total = e1r[8 * g]
        for m in range(1, 8):
            total = total + e1r[8 * g + m]
        halves.append(total)
    e2s[...] = jnp.concatenate(
        [
            halves[0][:, :KP],
            halves[1][:, :KP],
            halves[0][:, KP : 2 * KP],
            halves[1][:, KP : 2 * KP],
            halves[0][:, 2 * KP :] + halves[1][:, 2 * KP :],
        ],
        axis=1,
    )
    rows = along_stream(lambda p: e2s, e2r, e2ss, e2rs)
    start(rows)
    e2r[i] = e2s[...]
    arrive(rows)
    total = e2r[0][:, 2 * KP :]
    for s in range(1, NS):
        total = total + e2r[s][:, 2 * KP :]
    for s in range(NS):
        value = e2r[s]
        for g in range(2):
            upper[pl.ds(2 * s + g, 1), :] = value[:, g * KP : g * KP + COEF]
    for n in range(3):
        upper[pl.ds(2 * NS + n, 1), :] = total[:, n * KP : n * KP + COEF]

    for n in range(SWEEPS):
        halo_sent(n)
    for copies in (meta1, meta2, data1, data2, terms, rows):
        sent(copies)


def per_device(
    velocity, diffusion, advection, normals, tile_cell, tile_class, tile_leaf, tile_owner,
    source_expansion, translation, leaf_octant, node_octant, subtree_octant, cluster_octant, root_octant,
):
    smem = pl.BlockSpec(memory_space=pltpu.SMEM)
    vmem = pl.BlockSpec(memory_space=pltpu.VMEM)
    hbm = pl.BlockSpec(memory_space=pl.ANY)
    dma = pltpu.SemaphoreType.DMA
    rows = (SX + 2) * SLAB
    flow, leaves, upper = pl.pallas_call(
        kernel,
        out_shape=(
            jax.ShapeDtypeStruct((3, SX * SD, SPAN), F32),
            jax.ShapeDtypeStruct((LEAVES, COEF), F32),
            jax.ShapeDtypeStruct((2 * NS + 3, COEF), F32),
        ),
        in_specs=[smem] * 6 + [vmem] * 3 + [hbm] * 6,
        out_specs=(vmem, vmem, vmem),
        scratch_shapes=[
            pltpu.VMEM((3, SX, SD, SPAN), BF16),
            pltpu.VMEM((SX, SD, SPAN), BF16),
            pltpu.VMEM((SX, SD, SPAN), BF16),
            pltpu.VMEM((3, TILES, SPAN), BF16),
            pltpu.VMEM((8 * COEF, SPAN), BF16),
            pltpu.VMEM((8 * COEF, COEF - 2 * SPAN), F32),
            pltpu.VMEM((3, 8 * KR, SPAN), F32),
            pltpu.VMEM((8 * KR, SPAN), F32),
            pltpu.VMEM((KP, 8 * SPAN), BF16),
            pltpu.VMEM((8, KP, KP), BF16),
            pltpu.VMEM((8, KP, KP), BF16),
            pltpu.VMEM((3, rows, SPAN), F32),
            pltpu.VMEM((3, rows, SPAN), F32),
            pltpu.VMEM((SX * SD, SPAN), F32),
            pltpu.VMEM((SX * SD, SPAN), F32),
            pltpu.VMEM((SX * SD, SPAN), F32),
            pltpu.VMEM((SLOTS, TILES), BF16),
            pltpu.VMEM((SLOTS, SLOTS), BF16),
            pltpu.VMEM((8 * LEAVES, SLOTS), BF16),
            pltpu.VMEM((3, TILES, SPAN), F32),
            pltpu.VMEM((SPAN, SPAN), BF16),
            pltpu.VMEM((SWEEPS, 2, 3, SD, SPAN), BF16),
            pltpu.VMEM((SWEEPS, 2, 3, SD, SPAN), BF16),
            pltpu.VMEM((SWEEPS, 2, 3, SX, SPAN), BF16),
            pltpu.VMEM((SWEEPS, 2, 3, SX, SPAN), BF16),
            pltpu.VMEM((ND, 2 * NS, SPAN), BF16),
            pltpu.VMEM((ND, 2 * NS, SPAN), BF16),
            pltpu.VMEM((NS, 2 * ND, SPAN), BF16),
            pltpu.VMEM((NS, 2 * ND, SPAN), BF16),
            pltpu.VMEM((ND, 2 * NS, SPAN), BF16),
            pltpu.VMEM((ND, 2 * NS, SPAN), BF16),
            pltpu.VMEM((NS, 2 * ND, SPAN), BF16),
            pltpu.VMEM((NS, 2 * ND, SPAN), BF16),
            pltpu.VMEM((1, 3 * KP), F32),
            pltpu.VMEM((ND, 1, 3 * KP), F32),
            pltpu.VMEM((1, 5 * KP), F32),
            pltpu.VMEM((NS, 1, 5 * KP), F32),
            dma((8,)),
            dma((SWEEPS, 4)),
            dma((SWEEPS, 4)),
            dma((ND,)), dma((ND,)), dma((NS,)), dma((NS,)),
            dma((ND,)), dma((ND,)), dma((NS,)), dma((NS,)),
            dma((ND,)), dma((ND,)), dma((NS,)), dma((NS,)),
        ],
        compiler_params=pltpu.CompilerParams(
            collective_id=0, has_side_effects=True, vmem_limit_bytes=60 * 1024 * 1024
        ),
        cost_estimate=pl.CostEstimate(flops=10**8, bytes_accessed=12 * 10**6, transcendentals=0),
    )(
        tile_cell.reshape(1, TILES),
        leaf_octant.reshape(8, 8),
        node_octant.reshape(1, 8),
        subtree_octant.reshape(2, 8),
        cluster_octant,
        root_octant.reshape(1, 8),
        tile_owner.reshape(1, TILES),
        tile_class.reshape(1, TILES),
        tile_leaf.reshape(1, TILES),
        velocity,
        diffusion,
        advection,
        normals.reshape(3, TILES, SPAN),
        jnp.transpose(source_expansion, (2, 0, 1)).reshape(8 * COEF, SPAN),
        jnp.transpose(translation, (1, 0, 2)).reshape(8 * COEF, COEF),
    )
    return flow.reshape(3, SX, SD, SPAN), leaves.reshape(1, 1, LEAVES, COEF), upper


def solution(mesh):
    in_specs = (
        P(None, "stream", "depth", None),
        P("stream", "depth", None),
        P("stream", "depth", None),
        P("stream", "depth", None, None, None),
        P("stream", "depth", None),
        P("stream", "depth", None),
        P("stream", "depth", None),
        P("stream", "depth", None, None),
        P(),
        P(),
        P("stream", "depth", None, None),
        P("stream", "depth", None),
        P("stream", None, None),
        P(),
        P(),
    )
    out_specs = (P(None, "stream", "depth", None), P("stream", "depth", None, None), P())
    return jax.shard_map(
        per_device, mesh=mesh, in_specs=in_specs, out_specs=out_specs, check_vma=False
    )
```

```python
import functools

import jax
import jax.numpy as jnp
from jax import lax
from jax.experimental import pallas as pl
from jax.experimental.pallas import tpu as pltpu
from jax.sharding import PartitionSpec as P

MESH = pl.DeviceIdType.MESH
F32, BF16, I32 = jnp.float32, jnp.bfloat16, jnp.int32
SX, SD, SPAN, SWEEPS, TILES, COEF, LEAVES = 64, 48, 128, 4, 128, 289, 64
NS, ND = 8, 16
SLAB, LEAD = 64, 8
KP = 384
KR = 304
SLOTS = 2 * NS * ND
UNROLL = 16


def split(value):
    high = value.astype(BF16).astype(F32)
    return high, value - high


def dot(a, b):
    return jnp.dot(a, b, preferred_element_type=F32)


def dot_nt(a, b):
    return lax.dot_general(a, b, (((1,), (1,)), ((), ())), preferred_element_type=F32)


def iota(shape, dim):
    return lax.broadcasted_iota(I32, shape, dim)


def kernel(
    cell, loct, noct, soct, coct, roct,
    owner, cls, leaf,
    vel, dif, adv, nrm, exp, tr,
    flow, leaves, upper,
    velv, difv, advv, nrmv, expv, trv, tv, ef, et, wh, wl, qa, qb, al, ka, be,
    pmat, perm, gg, picked, order, beside,
    xs, xr, ds, dr, m1s, m1r, m2s, m2r, a1s, a1r, a2s, a2r, e1s, e1r, e2s, e2r,
    lsem, hss, hrs, m1ss, m1rs, m2ss, m2rs, a1ss, a1rs, a2ss, a2rs, e1ss, e1rs, e2ss, e2rs,
):
    i, j = lax.axis_index("stream"), lax.axis_index("depth")

    loads = [
        pltpu.make_async_copy(s, d, lsem.at[n])
        for n, (s, d) in enumerate(
            (
                (vel, velv),
                (dif, difv),
                (adv, advv),
                (nrm, nrmv),
                (exp, expv),
                (tr.at[:, pl.ds(0, SPAN)], tv.at[0, pl.ds(0, 8 * COEF), :]),
                (tr.at[:, pl.ds(SPAN, SPAN)], tv.at[1, pl.ds(0, 8 * COEF), :]),
                (tr.at[:, pl.ds(2 * SPAN, COEF - 2 * SPAN)], trv),
            )
        )
    ]
    for copy in loads:
        copy.start()

    barrier = pltpu.get_barrier_semaphore()
    for r in range(1, ND):
        pl.semaphore_signal(barrier, inc=1, device_id=(i, lax.rem(j + r, ND)), device_id_type=MESH)
    for r in range(1, NS):
        pl.semaphore_signal(barrier, inc=1, device_id=(lax.rem(i + r, NS), j), device_id_type=MESH)

    def along_depth(src, dst, ss, rs):
        return [
            pltpu.make_async_remote_copy(
                src_ref=src(lax.rem(j + r, ND)), dst_ref=dst.at[j], send_sem=ss.at[r], recv_sem=rs.at[r],
                device_id=(i, lax.rem(j + r, ND)), device_id_type=MESH,
            )
            for r in range(1, ND)
        ]

    def along_stream(src, dst, ss, rs):
        return [
            pltpu.make_async_remote_copy(
                src_ref=src(lax.rem(i + r, NS)), dst_ref=dst.at[i], send_sem=ss.at[r], recv_sem=rs.at[r],
                device_id=(lax.rem(i + r, NS), j), device_id_type=MESH,
            )
            for r in range(1, NS)
        ]

    def start(copies):
        for copy in copies:
            copy.start()

    def arrive(copies):
        for copy in copies:
            copy.wait_recv()

    def sent(copies):
        for copy in copies:
            copy.wait_send()

    def halo(n):
        xlow = velv.at[:, 0] if n == 0 else xs.at[n, 0]
        xhigh = velv.at[:, SX - 1] if n == 0 else xs.at[n, 1]

        def copy(src, dst, which, device):
            return pltpu.make_async_remote_copy(
                src_ref=src, dst_ref=dst, send_sem=hss.at[n, which], recv_sem=hrs.at[n, which],
                device_id=device, device_id_type=MESH,
            )

        return (
            (i < NS - 1, i > 0, copy(xhigh, xr.at[n, 0], 0, (lax.rem(i + 1, NS), j))),
            (i > 0, i < NS - 1, copy(xlow, xr.at[n, 1], 1, (lax.rem(i + NS - 1, NS), j))),
            (j < ND - 1, j > 0, copy(ds.at[n, 1], dr.at[n, 0], 2, (i, lax.rem(j + 1, ND)))),
            (j > 0, j < ND - 1, copy(ds.at[n, 0], dr.at[n, 1], 3, (i, lax.rem(j + ND - 1, ND)))),
        )

    def halo_start(n):
        for send, _, copy in halo(n):
            pl.when(send)(copy.start)

    def halo_arrive(n):
        for _, receive, copy in halo(n):
            pl.when(receive)(copy.wait_recv)

    def halo_sent(n):
        for send, _, copy in halo(n):
            pl.when(send)(copy.wait_send)

    for edge, ref, side in ((i == 0, xr, 0), (i == NS - 1, xr, 1), (j == 0, dr, 0), (j == ND - 1, dr, 1)):

        @pl.when(edge)
        def _(ref=ref, side=side):
            for n in range(SWEEPS):
                ref[n, side] = jnp.zeros(ref.shape[2:], BF16)

    zero8 = jnp.zeros((8, SPAN), F32)
    for q in (qa, qb):
        for k in range(3):
            for x in (0, SX + 1):
                q[k, pl.ds(x * SLAB, SLAB), :] = jnp.zeros((SLAB, SPAN), F32)

    def clear(x, carry):
        for q in (qa, qb):
            for k in range(3):
                q[k, pl.ds(pl.multiple_of(x * SLAB, 8), 8), :] = zero8
                q[k, pl.ds(pl.multiple_of(x * SLAB + LEAD + SD, 8), 8), :] = zero8
        return carry

    lax.fori_loop(1, SX + 1, clear, 0)

    own = owner[...]
    across = jnp.broadcast_to(own.astype(F32), (TILES, TILES))
    down = jnp.transpose(across)
    before = iota((TILES, TILES), 0) < iota((TILES, TILES), 1)
    rank = jnp.sum(jnp.where((across == down) & before, 1.0, 0.0), axis=0, keepdims=True).astype(I32)
    slot = (own & (ND - 1)) * (2 * NS) + (own >> 4) * 2 + rank
    pmat[...] = jnp.where(iota((SLOTS, TILES), 0) == slot, 1.0, 0.0).astype(BF16)
    feature = iota((SPAN, TILES), 0)
    meta = jnp.where((feature == leaf[...]) | (feature == cls[...] + LEAVES), 1.0, 0.0).astype(BF16)
    m1s[...] = dot_nt(pmat[...], meta).astype(BF16).reshape(ND, 2 * NS, SPAN)
    apart = (iota((SPAN, SPAN), 0) - iota((SPAN, SPAN), 1)) & (SPAN - 1)
    beside[...] = jnp.where((apart == 1) | (apart == SPAN - 1), 1.0, 0.0).astype(BF16)
    out = iota((SLOTS, SLOTS), 0)
    source = ((out >> 1) & (ND - 1)) * (2 * NS) + (out >> 5) * 2 + (out & 1)
    perm[...] = jnp.where(iota((SLOTS, SLOTS), 1) == source, 1.0, 0.0).astype(BF16)

    for copy in loads[:3]:
        copy.wait()

    def widen(x, carry):
        at = pl.multiple_of((x + 1) * SLAB + LEAD, 8)
        for k in range(3):
            qa[k, pl.ds(at, SD), :] = velv[k, x].astype(F32)
        kappa = difv[x].astype(F32)
        speed = advv[x].astype(F32)
        rows = pl.ds(pl.multiple_of(x * SD, 8), SD)
        ka[rows, :] = kappa
        be[rows, :] = kappa + speed
        al[rows, :] = 1.0 - 6.0 * kappa - speed
        return carry

    lax.fori_loop(0, SX, widen, 0)
    low = pl.ds(SLAB + LEAD, SX, stride=SLAB)
    high = pl.ds(SLAB + LEAD + SD - 1, SX, stride=SLAB)
    for k in range(3):
        ds[0, 0, k] = qa[k, low, :].astype(BF16)
        ds[0, 1, k] = qa[k, high, :].astype(BF16)

    pl.semaphore_wait(barrier, ND - 1 + NS - 1)
    halo_start(0)
    meta1 = along_depth(lambda p: m1s.at[p], m1r, m1ss, m1rs)
    start(meta1)
    m1r[j] = m1s[j]

    def sweep(src, dst, pitch, lead):
        slabs = src.reshape(3, SX + 2, SLAB, SPAN)

        def step(x, carry):
            rows = pl.ds(pl.multiple_of(x * SD, 8), SD)
            kappa, beta, alpha = ka[rows, :], be[rows, :], al[rows, :]
            for k in range(3):
                c = slabs[k, x + 1, pl.ds(LEAD, SD), :]
                f = slabs[k, x + 2, pl.ds(LEAD, SD), :]
                b = slabs[k, x, pl.ds(LEAD, SD), :]
                up = slabs[k, x + 1, pl.ds(LEAD + 1, SD), :]
                down = slabs[k, x + 1, pl.ds(LEAD - 1, SD), :]
                total = f + (up + down) + dot(c.astype(BF16), beside[...])
                dst[k, pl.ds(pl.multiple_of(x * pitch + lead, 8), SD), :] = alpha * c + kappa * total + beta * b
            return carry

        lax.fori_loop(0, SX, step, 0, unroll=UNROLL)

    def faces(n, dst, pitch, lead):
        first = pl.ds(lead, SD)
        last = pl.ds((SX - 1) * pitch + lead, SD)
        low = pl.ds(lead, SX, stride=pitch)
        high = pl.ds(lead + SD - 1, SX, stride=pitch)
        klow = ka[pl.ds(0, SX, stride=SD), :]
        khigh = ka[pl.ds(SD - 1, SX, stride=SD), :]
        for k in range(3):
            dst[k, first, :] = dst[k, first, :] + be[pl.ds(0, SD), :] * xr[n, 0, k].astype(F32)
            dst[k, last, :] = dst[k, last, :] + ka[pl.ds((SX - 1) * SD, SD), :] * xr[n, 1, k].astype(F32)
            ql = dst[k, low, :] + klow * dr[n, 0, k].astype(F32)
            qh = dst[k, high, :] + khigh * dr[n, 1, k].astype(F32)
            dst[k, low, :] = ql
            dst[k, high, :] = qh
            if n + 1 < SWEEPS:
                ds[n + 1, 0, k] = ql.astype(BF16)
                ds[n + 1, 1, k] = qh.astype(BF16)
                xs[n + 1, 0, k] = dst[k, first, :].astype(BF16)
                xs[n + 1, 1, k] = dst[k, last, :].astype(BF16)
        if n + 1 < SWEEPS:
            halo_start(n + 1)

    sweep(qa, qb, SLAB, SLAB + LEAD)
    for copy in loads[5:]:
        copy.wait()
    for w in (wh, wl):
        for o in range(8):
            w[o, pl.ds(KR, KP - KR), :] = jnp.zeros((KP - KR, KP), BF16)
    tv[:, pl.ds(8 * COEF, 8 * (KR - COEF)), :] = jnp.zeros((3, 8 * (KR - COEF), SPAN), F32)
    tv[2, pl.ds(0, 8 * COEF), :] = jnp.concatenate(
        [trv[...], jnp.zeros((8 * COEF, KP - COEF), F32)], axis=1
    )

    def halve(b, carry):
        for o in range(8):
            rows = pl.ds(b * 128 + o, 16, stride=8)
            to = pl.ds(pl.multiple_of(b * 16, 16), 16)
            for n in range(3):
                lanes = pl.ds(n * SPAN, SPAN)
                h, l = split(tv[n, rows, :])
                wh[o, to, lanes] = h.astype(BF16)
                wl[o, to, lanes] = l.astype(BF16)
        return carry

    lax.fori_loop(0, KR // 16, halve, 0)
    halo_arrive(0)
    faces(0, qb, SLAB, SLAB + LEAD)

    sweep(qb, qa, SLAB, SLAB + LEAD)
    arrive(meta1)
    m2s[...] = dot(perm[...], m1r[...].reshape(SLOTS, SPAN)).astype(BF16).reshape(NS, 2 * ND, SPAN)
    meta2 = along_stream(lambda p: m2s.at[p], m2r, m2ss, m2rs)
    start(meta2)
    m2r[i] = m2s[i]
    loads[4].wait()
    et[pl.ds(KR, KP - KR), :] = jnp.zeros((KP - KR, 8 * SPAN), BF16)
    ef[pl.ds(0, 8 * COEF), :] = expv[...].astype(F32)
    ef[pl.ds(8 * COEF, 8 * (KR - COEF)), :] = jnp.zeros((8 * (KR - COEF), SPAN), F32)

    def classes(b, carry):
        for c in range(8):
            value = ef[pl.ds(b * 128 + c, 16, stride=8), :]
            et[pl.ds(pl.multiple_of(b * 16, 16), 16), pl.ds(c * SPAN, SPAN)] = value.astype(BF16)
        return carry

    lax.fori_loop(0, KR // 16, classes, 0)
    halo_arrive(1)
    faces(1, qa, SLAB, SLAB + LEAD)

    sweep(qa, qb, SLAB, SLAB + LEAD)
    arrive(meta2)
    lane = iota((1, SPAN), 1)
    octant = jnp.full((1, SPAN), -1, I32)
    for l in range(LEAVES):
        octant = jnp.where(lane == l, loct[l // 8, l % 8], octant)
    row = iota((SPAN, SPAN), 0)
    ordered = jnp.where((row & 7) == (lane >> 3), jnp.where((row >> 3) == octant, 1.0, 0.0), 0.0)
    order[...] = jnp.transpose(ordered).astype(BF16)
    arrived = m2r[...].reshape(SLOTS, SPAN)
    leaf_of = dot_nt(ordered[:LEAVES].astype(BF16), arrived)
    pick = jnp.where(iota((8, SPAN), 1) == iota((8, SPAN), 0) + LEAVES, 1.0, 0.0).astype(BF16)
    class_of = dot_nt(pick, arrived)
    for c in range(8):
        gg[pl.ds(c * LEAVES, LEAVES), :] = (leaf_of * class_of[c : c + 1, :]).astype(BF16)
    halo_arrive(2)
    faces(2, qb, SLAB, SLAB + LEAD)

    sweep(qb, flow, SD, 0)
    halo_arrive(3)
    faces(3, flow, SD, 0)

    loads[3].wait()

    def sample(t, carry):
        for k in range(3):
            picked[k, t] = flow[k, cell[0, t]]
        return carry

    lax.fori_loop(0, TILES, sample, 0, unroll=8)
    strength = nrmv[0].astype(F32) * picked[0]
    for k in (1, 2):
        strength = strength + nrmv[k].astype(F32) * picked[k]
    a1s[...] = dot(pmat[...], strength.astype(BF16)).astype(BF16).reshape(ND, 2 * NS, SPAN)
    data1 = along_depth(lambda p: a1s.at[p], a1r, a1ss, a1rs)
    start(data1)
    a1r[j] = a1s[j]
    arrive(data1)
    a2s[...] = dot(perm[...], a1r[...].reshape(SLOTS, SPAN)).astype(BF16).reshape(NS, 2 * ND, SPAN)
    data2 = along_stream(lambda p: a2s.at[p], a2r, a2ss, a2rs)
    start(data2)
    a2r[i] = a2s[i]
    arrive(data2)

    sums = dot(gg[...], a2r[...].reshape(SLOTS, SPAN))
    blocks = []
    for c in range(8):
        h, l = split(sums[c * LEAVES : (c + 1) * LEAVES])
        blocks.append(jnp.concatenate([h, l], axis=0).astype(BF16))
    both = dot_nt(jnp.concatenate(blocks, axis=1), et[...])
    ordered_leaves = both[:LEAVES] + both[LEAVES:]

    h, l = split(ordered_leaves)
    lhs = jnp.concatenate(
        [jnp.concatenate([h[8 * o : 8 * o + 8], l[8 * o : 8 * o + 8]], axis=0).astype(BF16) for o in range(8)], axis=1
    )
    product = dot(lhs, wh[...].reshape(8 * KP, KP)) + dot(lhs, wl[...].reshape(8 * KP, KP))
    h, l = split(product[:8] + product[8:])
    node = iota((16, KP), 0) & 7
    octant = jnp.full((16, KP), -1, I32)
    for p in range(8):
        octant = jnp.where(node == p, noct[0, p], octant)
    stacked = jnp.concatenate([h, l], axis=0)
    lhs = jnp.concatenate([jnp.where(octant == o, stacked, 0.0).astype(BF16) for o in range(8)], axis=1)
    subtree = jnp.sum(dot(lhs, wh[...].reshape(8 * KP, KP)) + dot(lhs, wl[...].reshape(8 * KP, KP)), axis=0, keepdims=True)

    group, member = j >> 3, j & 7

    def lift(vector, which):
        h, l = split(vector)
        place = iota((16, KP), 0)
        rows = jnp.where(place == 0, h, jnp.where(place == 1, l, 0.0)).astype(BF16)
        return jnp.sum(dot(rows, wh[which]) + dot(rows, wl[which]), axis=0, keepdims=True)

    in_cluster = lift(subtree, soct[group, member])
    in_half = lift(in_cluster, coct[group, i])
    in_root = lift(in_half, roct[0, group])
    e1s[...] = jnp.concatenate([in_cluster, in_half, in_root], axis=1)
    terms = along_depth(lambda p: e1s, e1r, e1ss, e1rs)
    start(terms)
    e1r[j] = e1s[...]

    h, rest = split(ordered_leaves)
    m, l = split(rest)
    turn = order[:LEAVES, :LEAVES]
    leaves[...] = (dot(turn, h.astype(BF16)) + dot(turn, m.astype(BF16)) + dot(turn, l.astype(BF16)))[:, :COEF]

    arrive(terms)
    halves = []
    for g in range(2):
        total = e1r[8 * g]
        for m in range(1, 8):
            total = total + e1r[8 * g + m]
        halves.append(total)
    e2s[...] = jnp.concatenate(
        [
            halves[0][:, :KP],
            halves[1][:, :KP],
            halves[0][:, KP : 2 * KP],
            halves[1][:, KP : 2 * KP],
            halves[0][:, 2 * KP :] + halves[1][:, 2 * KP :],
        ],
        axis=1,
    )
    rows = along_stream(lambda p: e2s, e2r, e2ss, e2rs)
    start(rows)
    e2r[i] = e2s[...]
    arrive(rows)
    total = e2r[0][:, 2 * KP :]
    for s in range(1, NS):
        total = total + e2r[s][:, 2 * KP :]
    for s in range(NS):
        value = e2r[s]
        for g in range(2):
            upper[pl.ds(2 * s + g, 1), :] = value[:, g * KP : g * KP + COEF]
    for n in range(3):
        upper[pl.ds(2 * NS + n, 1), :] = total[:, n * KP : n * KP + COEF]

    for n in range(SWEEPS):
        halo_sent(n)
    for copies in (meta1, meta2, data1, data2, terms, rows):
        sent(copies)


def write_out(*refs):
    copies = [pltpu.make_async_copy(refs[n], refs[n + 3], refs[6].at[n]) for n in range(3)]
    for copy in copies:
        copy.start()
    for copy in copies:
        copy.wait()


def per_device(
    velocity, diffusion, advection, normals, tile_cell, tile_class, tile_leaf, tile_owner,
    source_expansion, translation, leaf_octant, node_octant, subtree_octant, cluster_octant, root_octant,
):
    smem = pl.BlockSpec(memory_space=pltpu.SMEM)
    vmem = pl.BlockSpec(memory_space=pltpu.VMEM)
    hbm = pl.BlockSpec(memory_space=pltpu.HBM)
    dma = pltpu.SemaphoreType.DMA
    rows = (SX + 2) * SLAB
    shapes = ((3, SX * SD, SPAN), (LEAVES, COEF), (2 * NS + 3, COEF))
    results = pl.pallas_call(
        kernel,
        out_shape=tuple(pltpu.VMEM(shape, F32) for shape in shapes),
        in_specs=[smem] * 6 + [vmem] * 3 + [hbm] * 6,
        out_specs=(vmem, vmem, vmem),
        scratch_shapes=[
            pltpu.VMEM((3, SX, SD, SPAN), BF16),
            pltpu.VMEM((SX, SD, SPAN), BF16),
            pltpu.VMEM((SX, SD, SPAN), BF16),
            pltpu.VMEM((3, TILES, SPAN), BF16),
            pltpu.VMEM((8 * COEF, SPAN), BF16),
            pltpu.VMEM((8 * COEF, COEF - 2 * SPAN), F32),
            pltpu.VMEM((3, 8 * KR, SPAN), F32),
            pltpu.VMEM((8 * KR, SPAN), F32),
            pltpu.VMEM((KP, 8 * SPAN), BF16),
            pltpu.VMEM((8, KP, KP), BF16),
            pltpu.VMEM((8, KP, KP), BF16),
            pltpu.VMEM((3, rows, SPAN), F32),
            pltpu.VMEM((3, rows, SPAN), F32),
            pltpu.VMEM((SX * SD, SPAN), F32),
            pltpu.VMEM((SX * SD, SPAN), F32),
            pltpu.VMEM((SX * SD, SPAN), F32),
            pltpu.VMEM((SLOTS, TILES), BF16),
            pltpu.VMEM((SLOTS, SLOTS), BF16),
            pltpu.VMEM((8 * LEAVES, SLOTS), BF16),
            pltpu.VMEM((3, TILES, SPAN), F32),
            pltpu.VMEM((SPAN, SPAN), BF16),
            pltpu.VMEM((SPAN, SPAN), BF16),
            pltpu.VMEM((SWEEPS, 2, 3, SD, SPAN), BF16),
            pltpu.VMEM((SWEEPS, 2, 3, SD, SPAN), BF16),
            pltpu.VMEM((SWEEPS, 2, 3, SX, SPAN), BF16),
            pltpu.VMEM((SWEEPS, 2, 3, SX, SPAN), BF16),
            pltpu.VMEM((ND, 2 * NS, SPAN), BF16),
            pltpu.VMEM((ND, 2 * NS, SPAN), BF16),
            pltpu.VMEM((NS, 2 * ND, SPAN), BF16),
            pltpu.VMEM((NS, 2 * ND, SPAN), BF16),
            pltpu.VMEM((ND, 2 * NS, SPAN), BF16),
            pltpu.VMEM((ND, 2 * NS, SPAN), BF16),
            pltpu.VMEM((NS, 2 * ND, SPAN), BF16),
            pltpu.VMEM((NS, 2 * ND, SPAN), BF16),
            pltpu.VMEM((1, 3 * KP), F32),
            pltpu.VMEM((ND, 1, 3 * KP), F32),
            pltpu.VMEM((1, 5 * KP), F32),
            pltpu.VMEM((NS, 1, 5 * KP), F32),
            dma((8,)),
            dma((SWEEPS, 4)),
            dma((SWEEPS, 4)),
            dma((ND,)), dma((ND,)), dma((NS,)), dma((NS,)),
            dma((ND,)), dma((ND,)), dma((NS,)), dma((NS,)),
            dma((ND,)), dma((ND,)), dma((NS,)), dma((NS,)),
        ],
        compiler_params=pltpu.CompilerParams(
            collective_id=0, has_side_effects=True, vmem_limit_bytes=60400 * 1024
        ),
        cost_estimate=pl.CostEstimate(flops=10**8, bytes_accessed=12 * 10**6, transcendentals=0),
    )(
        tile_cell.reshape(1, TILES),
        leaf_octant.reshape(8, 8),
        node_octant.reshape(1, 8),
        subtree_octant.reshape(2, 8),
        cluster_octant,
        root_octant.reshape(1, 8),
        tile_owner.reshape(1, TILES),
        tile_class.reshape(1, TILES),
        tile_leaf.reshape(1, TILES),
        velocity,
        diffusion,
        advection,
        normals.reshape(3, TILES, SPAN),
        jnp.transpose(source_expansion, (2, 0, 1)).reshape(8 * COEF, SPAN),
        jnp.transpose(translation, (1, 0, 2)).reshape(8 * COEF, COEF),
    )
    flow, leaves, upper = pl.pallas_call(
        write_out,
        out_shape=tuple(jax.ShapeDtypeStruct(shape, F32) for shape in shapes),
        in_specs=[vmem] * 3,
        out_specs=[hbm] * 3,
        scratch_shapes=[dma((3,))],
        compiler_params=pltpu.CompilerParams(vmem_limit_bytes=1024 * 1024),
    )(*results)
    return flow.reshape(3, SX, SD, SPAN), leaves.reshape(1, 1, LEAVES, COEF), upper


def solution(mesh):
    in_specs = (
        P(None, "stream", "depth", None),
        P("stream", "depth", None),
        P("stream", "depth", None),
        P("stream", "depth", None, None, None),
        P("stream", "depth", None),
        P("stream", "depth", None),
        P("stream", "depth", None),
        P("stream", "depth", None, None),
        P(),
        P(),
        P("stream", "depth", None, None),
        P("stream", "depth", None),
        P("stream", None, None),
        P(),
        P(),
    )
    out_specs = (P(None, "stream", "depth", None), P("stream", "depth", None, None), P())
    return jax.shard_map(
        per_device, mesh=mesh, in_specs=in_specs, out_specs=out_specs, check_vma=False
    )
```

```python
import functools

import jax
import jax.numpy as jnp
from jax import lax
from jax.experimental import pallas as pl
from jax.experimental.pallas import tpu as pltpu
from jax.sharding import PartitionSpec as P

MESH = pl.DeviceIdType.MESH
F32, BF16, I32 = jnp.float32, jnp.bfloat16, jnp.int32
SX, SD, SPAN, SWEEPS, TILES, COEF, LEAVES = 64, 48, 128, 4, 128, 289, 64
NS, ND = 8, 16
SLAB, LEAD = 64, 8
KP = 384
KR = 304
SLOTS = 2 * NS * ND
UNROLL = 16
PARTS = 2


def split(value):
    high = value.astype(BF16).astype(F32)
    return high, value - high


def dot(a, b):
    return jnp.dot(a, b, preferred_element_type=F32)


def dot_nt(a, b):
    return lax.dot_general(a, b, (((1,), (1,)), ((), ())), preferred_element_type=F32)


DEPTH_ORDER = (10, 9, 11, 6, 14, 5, 7, 13, 15, 8, 2, 4, 12, 1, 3)
STREAM_ORDER = (5, 4, 3, 7, 2, 6, 1)


def flip(value, bits):
    if bits == 0:
        return value
    if bits == 1:
        return value + 1 - 2 * lax.rem(value, 2)
    if bits == 2:
        return lax.rem(value + 2, 4)
    return 3 - value


def iota(shape, dim):
    return lax.broadcasted_iota(I32, shape, dim)


def kernel(
    cell_in, loct_in, noct_in, soct_in, coct_in, roct_in, owner_in, cls_in, leaf_in,
    vel, dif, adv, nrm, exp, tr,
    flow, leaves, upper,
    cell, loct, noct, soct, coct, roct, owner, cls, leaf,
    velv, difv, advv, nrmv, expv, trv, tv, ef, et, wh, wl, qa, qb, al, ka, be,
    pmat, perm, gg, picked, order, beside, lifth, liftl,
    xs, xr, ds, dr, m1s, m1r, m2s, m2r, a1s, a1r, a2s, a2r, e1s, e1r, e2s, e2r,
    fsem, lsem, hss, hrs, m1ss, m1rs, m2ss, m2rs, a1ss, a1rs, a2ss, a2rs, e1ss, e1rs, e2ss, e2rs,
):
    i, j = lax.axis_index("stream"), lax.axis_index("depth")

    def in_depth(r):
        return 4 * flip(lax.div(j, 4), r // 4) + flip(lax.rem(j, 4), r % 4)

    def in_stream(r):
        core = lax.rem(i, 2)
        return 2 * flip(lax.div(i, 2), r // 2) + (1 - core if r % 2 else core)

    barrier = pltpu.get_barrier_semaphore()
    for r in DEPTH_ORDER:
        pl.semaphore_signal(barrier, inc=1, device_id=(i, in_depth(r)), device_id_type=MESH)
    for r in STREAM_ORDER:
        pl.semaphore_signal(barrier, inc=1, device_id=(in_stream(r), j), device_id_type=MESH)

    def part(src, dst, n, p):
        rows = pl.ds(p * (SX // PARTS), SX // PARTS)
        at = (slice(None), rows) if len(src.shape) == 4 else (rows,)
        return pltpu.make_async_copy(src.at[at], dst.at[at], fsem.at[n, p])

    field_loads = [
        [part(s, d, n, p) for n, (s, d) in enumerate(((vel, velv), (dif, difv), (adv, advv)))] for p in range(PARTS)
    ]
    for copies in field_loads:
        for copy in copies:
            copy.start()

    def along_depth(src, dst, ss, rs):
        return [
            pltpu.make_async_remote_copy(
                src_ref=src(in_depth(r)), dst_ref=dst.at[j], send_sem=ss.at[r], recv_sem=rs.at[r],
                device_id=(i, in_depth(r)), device_id_type=MESH,
            )
            for r in DEPTH_ORDER
        ]

    def along_stream(src, dst, ss, rs):
        return [
            pltpu.make_async_remote_copy(
                src_ref=src(in_stream(r)), dst_ref=dst.at[i], send_sem=ss.at[r], recv_sem=rs.at[r],
                device_id=(in_stream(r), j), device_id_type=MESH,
            )
            for r in STREAM_ORDER
        ]

    def start(copies):
        for copy in copies:
            copy.start()

    def arrive(copies):
        for copy in copies:
            copy.wait_recv()

    def sent(copies):
        for copy in copies:
            copy.wait_send()

    def halo(n, k):
        xlow = velv.at[k, 0] if n == 0 else xs.at[n, 0, k]
        xhigh = velv.at[k, SX - 1] if n == 0 else xs.at[n, 1, k]

        def copy(src, dst, which, device):
            return pltpu.make_async_remote_copy(
                src_ref=src, dst_ref=dst, send_sem=hss.at[n, which, k], recv_sem=hrs.at[n, which, k],
                device_id=device, device_id_type=MESH,
            )

        return (
            (j < ND - 1, j > 0, copy(ds.at[n, 1, k], dr.at[n, 0, k], 2, (i, lax.rem(j + 1, ND)))),
            (j > 0, j < ND - 1, copy(ds.at[n, 0, k], dr.at[n, 1, k], 3, (i, lax.rem(j + ND - 1, ND)))),
            (i < NS - 1, i > 0, copy(xhigh, xr.at[n, 0, k], 0, (lax.rem(i + 1, NS), j))),
            (i > 0, i < NS - 1, copy(xlow, xr.at[n, 1, k], 1, (lax.rem(i + NS - 1, NS), j))),
        )

    def halo_start(n, k):
        for send, _, copy in halo(n, k):
            pl.when(send)(copy.start)

    def halo_arrive(n, k):
        for _, receive, copy in halo(n, k):
            pl.when(receive)(copy.wait_recv)

    def halo_sent(n):
        for k in range(3):
            for send, _, copy in halo(n, k):
                pl.when(send)(copy.wait_send)

    for edge, ref, side in ((i == 0, xr, 0), (i == NS - 1, xr, 1), (j == 0, dr, 0), (j == ND - 1, dr, 1)):

        @pl.when(edge)
        def _(ref=ref, side=side):
            for n in range(SWEEPS):
                ref[n, side] = jnp.zeros(ref.shape[2:], BF16)

    zero8 = jnp.zeros((8, SPAN), F32)
    for q in (qa, qb):
        for k in range(3):
            for x in (0, SX + 1):
                q[k, pl.ds(x * SLAB, SLAB), :] = jnp.zeros((SLAB, SPAN), F32)

    def clear(x, carry):
        for q in (qa, qb):
            for k in range(3):
                q[k, pl.ds(pl.multiple_of(x * SLAB, 8), 8), :] = zero8
                q[k, pl.ds(pl.multiple_of(x * SLAB + LEAD + SD, 8), 8), :] = zero8
        return carry

    lax.fori_loop(1, SX + 1, clear, 0)

    apart = (iota((SPAN, SPAN), 0) - iota((SPAN, SPAN), 1)) & (SPAN - 1)
    beside[...] = jnp.where((apart == 1) | (apart == SPAN - 1), 1.0, 0.0).astype(BF16)


    def widen(x, carry):
        at = pl.multiple_of((x + 1) * SLAB + LEAD, 8)
        for k in range(3):
            qa[k, pl.ds(at, SD), :] = velv[k, x].astype(F32)
        kappa = difv[x].astype(F32)
        speed = advv[x].astype(F32)
        rows = pl.ds(pl.multiple_of(x * SD, 8), SD)
        ka[rows, :] = kappa
        be[rows, :] = kappa + speed
        al[rows, :] = 1.0 - 6.0 * kappa - speed
        return carry

    for p, copies in enumerate(field_loads):
        for copy in copies:
            copy.wait()
        lax.fori_loop(p * (SX // PARTS), (p + 1) * (SX // PARTS), widen, 0, unroll=4)
    loads = [
        pltpu.make_async_copy(s, d, lsem.at[n])
        for n, (s, d) in enumerate(
            (
                (owner_in, owner),
                (cls_in, cls),
                (leaf_in, leaf),
                (cell_in, cell),
                (loct_in, loct),
                (noct_in, noct),
                (soct_in, soct),
                (coct_in, coct),
                (roct_in, roct),
                (nrm, nrmv),
                (exp, expv),
                (tr.at[:, pl.ds(0, SPAN)], tv.at[0, pl.ds(0, 8 * COEF), :]),
                (tr.at[:, pl.ds(SPAN, SPAN)], tv.at[1, pl.ds(0, 8 * COEF), :]),
                (tr.at[:, pl.ds(2 * SPAN, COEF - 2 * SPAN)], trv),
            )
        )
    ]
    low = pl.ds(SLAB + LEAD, SX, stride=SLAB)
    high = pl.ds(SLAB + LEAD + SD - 1, SX, stride=SLAB)
    for k in range(3):
        ds[0, 0, k] = qa[k, low, :].astype(BF16)
        ds[0, 1, k] = qa[k, high, :].astype(BF16)

    pl.semaphore_wait(barrier, ND - 1 + NS - 1)
    for k in range(3):
        halo_start(0, k)
    for copy in loads:
        copy.start()

    for copy in loads[:9]:
        copy.wait()
    own = owner[...]
    across = jnp.broadcast_to(own.astype(F32), (TILES, TILES))
    down = jnp.transpose(across)
    before = iota((TILES, TILES), 0) < iota((TILES, TILES), 1)
    rank = jnp.sum(jnp.where((across == down) & before, 1.0, 0.0), axis=0, keepdims=True).astype(I32)
    slot = (own & (ND - 1)) * (2 * NS) + (own >> 4) * 2 + rank
    pmat[...] = jnp.where(iota((SLOTS, TILES), 0) == slot, 1.0, 0.0).astype(BF16)
    feature = iota((SPAN, TILES), 0)
    meta = jnp.where((feature == leaf[...]) | (feature == cls[...] + LEAVES), 1.0, 0.0).astype(BF16)
    m1s[...] = dot_nt(pmat[...], meta).astype(BF16).reshape(ND, 2 * NS, SPAN)
    out = iota((SLOTS, SLOTS), 0)
    source = ((out >> 1) & (ND - 1)) * (2 * NS) + (out >> 5) * 2 + (out & 1)
    perm[...] = jnp.where(iota((SLOTS, SLOTS), 1) == source, 1.0, 0.0).astype(BF16)

    meta1 = along_depth(lambda p: m1s.at[p], m1r, m1ss, m1rs)
    start(meta1)
    m1r[j] = m1s[j]

    def sweep(src, dst, pitch, lead):
        slabs = src.reshape(3, SX + 2, SLAB, SPAN)

        def step(x, carry):
            rows = pl.ds(pl.multiple_of(x * SD, 8), SD)
            kappa, beta, alpha = ka[rows, :], be[rows, :], al[rows, :]
            for k in range(3):
                c = slabs[k, x + 1, pl.ds(LEAD, SD), :]
                f = slabs[k, x + 2, pl.ds(LEAD, SD), :]
                b = slabs[k, x, pl.ds(LEAD, SD), :]
                up = slabs[k, x + 1, pl.ds(LEAD + 1, SD), :]
                down = slabs[k, x + 1, pl.ds(LEAD - 1, SD), :]
                total = f + (up + down) + dot(c.astype(BF16), beside[...])
                dst[k, pl.ds(pl.multiple_of(x * pitch + lead, 8), SD), :] = alpha * c + kappa * total + beta * b
            return carry

        lax.fori_loop(0, SX, step, 0, unroll=UNROLL)

    def faces(n, dst, pitch, lead):
        first = pl.ds(lead, SD)
        last = pl.ds((SX - 1) * pitch + lead, SD)
        low = pl.ds(lead, SX, stride=pitch)
        high = pl.ds(lead + SD - 1, SX, stride=pitch)
        klow = ka[pl.ds(0, SX, stride=SD), :]
        khigh = ka[pl.ds(SD - 1, SX, stride=SD), :]
        for k in range(3):
            halo_arrive(n, k)
            qf = dst[k, first, :] + be[pl.ds(0, SD), :] * xr[n, 0, k].astype(F32)
            ql = dst[k, last, :] + ka[pl.ds((SX - 1) * SD, SD), :] * xr[n, 1, k].astype(F32)
            dst[k, first, :] = qf
            dst[k, last, :] = ql
            ql = dst[k, low, :] + klow * dr[n, 0, k].astype(F32)
            qh = dst[k, high, :] + khigh * dr[n, 1, k].astype(F32)
            dst[k, low, :] = ql
            dst[k, high, :] = qh
            if n + 1 < SWEEPS:
                ds[n + 1, 0, k] = ql.astype(BF16)
                ds[n + 1, 1, k] = qh.astype(BF16)
                xs[n + 1, 0, k] = dst[k, first, :].astype(BF16)
                xs[n + 1, 1, k] = dst[k, last, :].astype(BF16)
                halo_start(n + 1, k)

    sweep(qa, qb, SLAB, SLAB + LEAD)
    faces(0, qb, SLAB, SLAB + LEAD)

    sweep(qb, qa, SLAB, SLAB + LEAD)
    arrive(meta1)
    m2s[...] = dot(perm[...], m1r[...].reshape(SLOTS, SPAN)).astype(BF16).reshape(NS, 2 * ND, SPAN)
    meta2 = along_stream(lambda p: m2s.at[p], m2r, m2ss, m2rs)
    start(meta2)
    m2r[i] = m2s[i]
    faces(1, qa, SLAB, SLAB + LEAD)

    sweep(qa, qb, SLAB, SLAB + LEAD)
    faces(2, qb, SLAB, SLAB + LEAD)

    sweep(qb, flow, SD, 0)
    faces(3, flow, SD, 0)

    loads[9].wait()

    def sample(t, carry):
        for k in range(3):
            picked[k, t] = flow[k, cell[0, t]]
        return carry

    lax.fori_loop(0, TILES, sample, 0, unroll=8)
    strength = nrmv[0].astype(F32) * picked[0]
    for k in (1, 2):
        strength = strength + nrmv[k].astype(F32) * picked[k]
    a1s[...] = dot(pmat[...], strength.astype(BF16)).astype(BF16).reshape(ND, 2 * NS, SPAN)
    data1 = along_depth(lambda p: a1s.at[p], a1r, a1ss, a1rs)
    start(data1)
    a1r[j] = a1s[j]

    loads[10].wait()
    et[pl.ds(KR, KP - KR), :] = jnp.zeros((KP - KR, 8 * SPAN), BF16)
    ef[pl.ds(0, 8 * COEF), :] = expv[...].astype(F32)
    ef[pl.ds(8 * COEF, 8 * (KR - COEF)), :] = jnp.zeros((8 * (KR - COEF), SPAN), F32)

    def classes(b, carry):
        for c in range(8):
            value = ef[pl.ds(b * 128 + c, 16, stride=8), :]
            et[pl.ds(pl.multiple_of(b * 16, 16), 16), pl.ds(c * SPAN, SPAN)] = value.astype(BF16)
        return carry

    lax.fori_loop(0, KR // 16, classes, 0)
    for copy in loads[11:]:
        copy.wait()
    for w in (wh, wl):
        for o in range(8):
            w[o, pl.ds(KR, KP - KR), :] = jnp.zeros((KP - KR, KP), BF16)
    tv[:, pl.ds(8 * COEF, 8 * (KR - COEF)), :] = jnp.zeros((3, 8 * (KR - COEF), SPAN), F32)
    tv[2, pl.ds(0, 8 * COEF), :] = jnp.concatenate(
        [trv[...], jnp.zeros((8 * COEF, KP - COEF), F32)], axis=1
    )

    def halve(b, carry):
        for o in range(8):
            rows = pl.ds(b * 128 + o, 16, stride=8)
            to = pl.ds(pl.multiple_of(b * 16, 16), 16)
            for n in range(3):
                lanes = pl.ds(n * SPAN, SPAN)
                h, l = split(tv[n, rows, :])
                wh[o, to, lanes] = h.astype(BF16)
                wl[o, to, lanes] = l.astype(BF16)
        return carry

    lax.fori_loop(0, KR // 16, halve, 0)
    arrive(meta2)
    lane = iota((1, SPAN), 1)
    octant = jnp.full((1, SPAN), -1, I32)
    for l in range(LEAVES):
        octant = jnp.where(lane == l, loct[l // 8, l % 8], octant)
    row = iota((SPAN, SPAN), 0)
    ordered = jnp.where((row & 7) == (lane >> 3), jnp.where((row >> 3) == octant, 1.0, 0.0), 0.0)
    order[...] = jnp.transpose(ordered).astype(BF16)
    arrived = m2r[...].reshape(SLOTS, SPAN)
    leaf_of = dot_nt(ordered[:LEAVES].astype(BF16), arrived)
    pick = jnp.where(iota((8, SPAN), 1) == iota((8, SPAN), 0) + LEAVES, 1.0, 0.0).astype(BF16)
    class_of = dot_nt(pick, arrived)
    for c in range(8):
        gg[pl.ds(c * LEAVES, LEAVES), :] = (leaf_of * class_of[c : c + 1, :]).astype(BF16)
    arrive(data1)
    a2s[...] = dot(perm[...], a1r[...].reshape(SLOTS, SPAN)).astype(BF16).reshape(NS, 2 * ND, SPAN)
    data2 = along_stream(lambda p: a2s.at[p], a2r, a2ss, a2rs)
    start(data2)
    a2r[i] = a2s[i]

    group, member = lax.div(j, 8), lax.rem(j, 8)
    table = soct[group, member]
    high, low = wh[table], wl[table]
    lifth[:, :KP] = high
    liftl[:, :KP] = low
    for n, table in ((1, coct[group, i]), (2, roct[0, group])):
        following = wh[table]
        h, l = split(dot(high, following) + dot(low, following) + dot(high, wl[table]))
        high, low = h.astype(BF16), l.astype(BF16)
        lifth[:, pl.ds(n * KP, KP)] = high
        liftl[:, pl.ds(n * KP, KP)] = low
    arrive(data2)

    sums = dot(gg[...], a2r[...].reshape(SLOTS, SPAN))
    blocks = []
    for c in range(8):
        h, l = split(sums[c * LEAVES : (c + 1) * LEAVES])
        blocks.append(jnp.concatenate([h, l], axis=0).astype(BF16))
    both = dot_nt(jnp.concatenate(blocks, axis=1), et[...])
    ordered_leaves = both[:LEAVES] + both[LEAVES:]

    h, l = split(ordered_leaves)
    lhs = jnp.concatenate(
        [jnp.concatenate([h[8 * o : 8 * o + 8], l[8 * o : 8 * o + 8]], axis=0).astype(BF16) for o in range(8)], axis=1
    )
    product = dot(lhs, wh[...].reshape(8 * KP, KP)) + dot(lhs, wl[...].reshape(8 * KP, KP))
    h, l = split(product[:8] + product[8:])
    node = iota((16, KP), 0) & 7
    octant = jnp.full((16, KP), -1, I32)
    for p in range(8):
        octant = jnp.where(node == p, noct[0, p], octant)
    stacked = jnp.concatenate([h, l], axis=0)
    lhs = jnp.concatenate([jnp.where(octant == o, stacked, 0.0).astype(BF16) for o in range(8)], axis=1)
    subtree = jnp.sum(dot(lhs, wh[...].reshape(8 * KP, KP)) + dot(lhs, wl[...].reshape(8 * KP, KP)), axis=0, keepdims=True)

    h, l = split(subtree)
    place = iota((16, KP), 0)
    lhs = jnp.where(place == 0, h, jnp.where(place == 1, l, 0.0)).astype(BF16)
    e1s[...] = jnp.sum(dot(lhs, lifth[...]) + dot(lhs, liftl[...]), axis=0, keepdims=True)
    terms = along_depth(lambda p: e1s, e1r, e1ss, e1rs)
    start(terms)
    e1r[j] = e1s[...]

    h, rest = split(ordered_leaves)
    m, l = split(rest)
    turn = order[:LEAVES, :LEAVES]
    leaves[...] = (dot(turn, h.astype(BF16)) + dot(turn, m.astype(BF16)) + dot(turn, l.astype(BF16)))[:, :COEF]

    arrive(terms)
    halves = []
    for g in range(2):
        total = e1r[8 * g]
        for m in range(1, 8):
            total = total + e1r[8 * g + m]
        halves.append(total)
    e2s[...] = jnp.concatenate(
        [
            halves[0][:, :KP],
            halves[1][:, :KP],
            halves[0][:, KP : 2 * KP],
            halves[1][:, KP : 2 * KP],
            halves[0][:, 2 * KP :] + halves[1][:, 2 * KP :],
        ],
        axis=1,
    )
    rows = along_stream(lambda p: e2s, e2r, e2ss, e2rs)
    start(rows)
    e2r[i] = e2s[...]
    arrive(rows)
    total = e2r[0][:, 2 * KP :]
    for s in range(1, NS):
        total = total + e2r[s][:, 2 * KP :]
    for s in range(NS):
        value = e2r[s]
        for g in range(2):
            upper[pl.ds(2 * s + g, 1), :] = value[:, g * KP : g * KP + COEF]
    for n in range(3):
        upper[pl.ds(2 * NS + n, 1), :] = total[:, n * KP : n * KP + COEF]

    for n in range(SWEEPS):
        halo_sent(n)
    for copies in (meta1, meta2, data1, data2, terms, rows):
        sent(copies)


def write_out(*refs):
    copies = [pltpu.make_async_copy(refs[n], refs[n + 3], refs[6].at[n]) for n in range(3)]
    for copy in copies:
        copy.start()
    for copy in copies:
        copy.wait()


def per_device(
    velocity, diffusion, advection, normals, tile_cell, tile_class, tile_leaf, tile_owner,
    source_expansion, translation, leaf_octant, node_octant, subtree_octant, cluster_octant, root_octant,
):
    vmem = pl.BlockSpec(memory_space=pltpu.VMEM)
    hbm = pl.BlockSpec(memory_space=pltpu.HBM)
    dma = pltpu.SemaphoreType.DMA
    rows = (SX + 2) * SLAB
    shapes = ((3, SX * SD, SPAN), (LEAVES, COEF), (2 * NS + 3, COEF))
    results = pl.pallas_call(
        kernel,
        out_shape=tuple(pltpu.VMEM(shape, F32) for shape in shapes),
        in_specs=[hbm] * 15,
        out_specs=(vmem, vmem, vmem),
        scratch_shapes=[
            pltpu.SMEM((1, TILES), I32),
            pltpu.SMEM((8, 8), I32),
            pltpu.SMEM((1, 8), I32),
            pltpu.SMEM((2, 8), I32),
            pltpu.SMEM((2, 8), I32),
            pltpu.SMEM((1, 8), I32),
            pltpu.VMEM((1, TILES), I32),
            pltpu.VMEM((1, TILES), I32),
            pltpu.VMEM((1, TILES), I32),
            pltpu.VMEM((3, SX, SD, SPAN), BF16),
            pltpu.VMEM((SX, SD, SPAN), BF16),
            pltpu.VMEM((SX, SD, SPAN), BF16),
            pltpu.VMEM((3, TILES, SPAN), BF16),
            pltpu.VMEM((8 * COEF, SPAN), BF16),
            pltpu.VMEM((8 * COEF, COEF - 2 * SPAN), F32),
            pltpu.VMEM((3, 8 * KR, SPAN), F32),
            pltpu.VMEM((8 * KR, SPAN), F32),
            pltpu.VMEM((KP, 8 * SPAN), BF16),
            pltpu.VMEM((8, KP, KP), BF16),
            pltpu.VMEM((8, KP, KP), BF16),
            pltpu.VMEM((3, rows, SPAN), F32),
            pltpu.VMEM((3, rows, SPAN), F32),
            pltpu.VMEM((SX * SD, SPAN), F32),
            pltpu.VMEM((SX * SD, SPAN), F32),
            pltpu.VMEM((SX * SD, SPAN), F32),
            pltpu.VMEM((SLOTS, TILES), BF16),
            pltpu.VMEM((SLOTS, SLOTS), BF16),
            pltpu.VMEM((8 * LEAVES, SLOTS), BF16),
            pltpu.VMEM((3, TILES, SPAN), F32),
            pltpu.VMEM((SPAN, SPAN), BF16),
            pltpu.VMEM((SPAN, SPAN), BF16),
            pltpu.VMEM((KP, 3 * KP), BF16),
            pltpu.VMEM((KP, 3 * KP), BF16),
            pltpu.VMEM((SWEEPS, 2, 3, SD, SPAN), BF16),
            pltpu.VMEM((SWEEPS, 2, 3, SD, SPAN), BF16),
            pltpu.VMEM((SWEEPS, 2, 3, SX, SPAN), BF16),
            pltpu.VMEM((SWEEPS, 2, 3, SX, SPAN), BF16),
            pltpu.VMEM((ND, 2 * NS, SPAN), BF16),
            pltpu.VMEM((ND, 2 * NS, SPAN), BF16),
            pltpu.VMEM((NS, 2 * ND, SPAN), BF16),
            pltpu.VMEM((NS, 2 * ND, SPAN), BF16),
            pltpu.VMEM((ND, 2 * NS, SPAN), BF16),
            pltpu.VMEM((ND, 2 * NS, SPAN), BF16),
            pltpu.VMEM((NS, 2 * ND, SPAN), BF16),
            pltpu.VMEM((NS, 2 * ND, SPAN), BF16),
            pltpu.VMEM((1, 3 * KP), F32),
            pltpu.VMEM((ND, 1, 3 * KP), F32),
            pltpu.VMEM((1, 5 * KP), F32),
            pltpu.VMEM((NS, 1, 5 * KP), F32),
            dma((3, PARTS)),
            dma((14,)),
            dma((SWEEPS, 4, 3)),
            dma((SWEEPS, 4, 3)),
            dma((ND,)), dma((ND,)), dma((NS,)), dma((NS,)),
            dma((ND,)), dma((ND,)), dma((NS,)), dma((NS,)),
            dma((ND,)), dma((ND,)), dma((NS,)), dma((NS,)),
        ],
        compiler_params=pltpu.CompilerParams(
            collective_id=0, has_side_effects=True, vmem_limit_bytes=60400 * 1024
        ),
        cost_estimate=pl.CostEstimate(flops=10**8, bytes_accessed=12 * 10**6, transcendentals=0),
    )(
        tile_cell.reshape(1, TILES),
        leaf_octant.reshape(8, 8),
        node_octant.reshape(1, 8),
        subtree_octant.reshape(2, 8),
        cluster_octant,
        root_octant.reshape(1, 8),
        tile_owner.reshape(1, TILES),
        tile_class.reshape(1, TILES),
        tile_leaf.reshape(1, TILES),
        velocity,
        diffusion,
        advection,
        normals.reshape(3, TILES, SPAN),
        jnp.transpose(source_expansion, (2, 0, 1)).reshape(8 * COEF, SPAN),
        jnp.transpose(translation, (1, 0, 2)).reshape(8 * COEF, COEF),
    )
    flow, leaves, upper = pl.pallas_call(
        write_out,
        out_shape=tuple(jax.ShapeDtypeStruct(shape, F32) for shape in shapes),
        in_specs=[vmem] * 3,
        out_specs=[hbm] * 3,
        scratch_shapes=[dma((3,))],
        compiler_params=pltpu.CompilerParams(vmem_limit_bytes=1024 * 1024),
    )(*results)
    return flow.reshape(3, SX, SD, SPAN), leaves.reshape(1, 1, LEAVES, COEF), upper


def solution(mesh):
    in_specs = (
        P(None, "stream", "depth", None),
        P("stream", "depth", None),
        P("stream", "depth", None),
        P("stream", "depth", None, None, None),
        P("stream", "depth", None),
        P("stream", "depth", None),
        P("stream", "depth", None),
        P("stream", "depth", None, None),
        P(),
        P(),
        P("stream", "depth", None, None),
        P("stream", "depth", None),
        P("stream", None, None),
        P(),
        P(),
    )
    out_specs = (P(None, "stream", "depth", None), P("stream", "depth", None, None), P())
    return jax.shard_map(
        per_device, mesh=mesh, in_specs=in_specs, out_specs=out_specs, check_vma=False
    )
```

```python
import functools

import jax
import jax.numpy as jnp
from jax import lax
from jax.experimental import pallas as pl
from jax.experimental.pallas import tpu as pltpu
from jax.sharding import PartitionSpec as P

MESH = pl.DeviceIdType.MESH
F32, BF16, I32 = jnp.float32, jnp.bfloat16, jnp.int32
SX, SD, SPAN, SWEEPS, TILES, COEF, LEAVES = 64, 48, 128, 4, 128, 289, 64
NS, ND = 8, 16
SLAB, LEAD = 64, 8
KP = 384
KR = 304
SLOTS = 2 * NS * ND
UNROLL = 16
PARTS = 2


def split(value):
    high = value.astype(BF16).astype(F32)
    return high, value - high


def dot(a, b):
    return jnp.dot(a, b, preferred_element_type=F32)


def dot_nt(a, b):
    return lax.dot_general(a, b, (((1,), (1,)), ((), ())), preferred_element_type=F32)


DEPTH_ORDER = (10, 9, 11, 6, 14, 5, 7, 13, 15, 8, 2, 4, 12, 1, 3)
STREAM_ORDER = (5, 4, 3, 7, 2, 6, 1)


def flip(value, bits):
    if bits == 0:
        return value
    if bits == 1:
        return value + 1 - 2 * lax.rem(value, 2)
    if bits == 2:
        return lax.rem(value + 2, 4)
    return 3 - value


def iota(shape, dim):
    return lax.broadcasted_iota(I32, shape, dim)


def kernel(
    cell_in, loct_in, noct_in, soct_in, coct_in, roct_in, owner_in, cls_in, leaf_in,
    vel, dif, adv, nrm, exp, tr,
    flow, leaves, upper,
    cell, loct, noct, soct, coct, roct, owner, cls, leaf,
    velv, difv, advv, nrmv, expv, trv, tv, ef, et, w, qa, qb, al, ka, be,
    pmat, perm, gg, picked, order, beside, lifts,
    xs, xr, ds, dr, m1s, m1r, m2s, m2r, a1s, a1r, a2s, a2r, e1s, e1r, e2s, e2r,
    fsem, lsem, hss, hrs, m1ss, m1rs, m2ss, m2rs, a1ss, a1rs, a2ss, a2rs, e1ss, e1rs, e2ss, e2rs,
):
    i, j = lax.axis_index("stream"), lax.axis_index("depth")

    def in_depth(r):
        return 4 * flip(lax.div(j, 4), r // 4) + flip(lax.rem(j, 4), r % 4)

    def in_stream(r):
        core = lax.rem(i, 2)
        return 2 * flip(lax.div(i, 2), r // 2) + (1 - core if r % 2 else core)

    barrier = pltpu.get_barrier_semaphore()
    for r in DEPTH_ORDER:
        pl.semaphore_signal(barrier, inc=1, device_id=(i, in_depth(r)), device_id_type=MESH)
    for r in STREAM_ORDER:
        pl.semaphore_signal(barrier, inc=1, device_id=(in_stream(r), j), device_id_type=MESH)

    def part(src, dst, n, p):
        rows = pl.ds(p * (SX // PARTS), SX // PARTS)
        at = (slice(None), rows) if len(src.shape) == 4 else (rows,)
        return pltpu.make_async_copy(src.at[at], dst.at[at], fsem.at[n, p])

    field_loads = [
        [part(s, d, n, p) for n, (s, d) in enumerate(((vel, velv), (dif, difv), (adv, advv)))] for p in range(PARTS)
    ]
    for copies in field_loads:
        for copy in copies:
            copy.start()

    def along_depth(src, dst, ss, rs):
        return [
            pltpu.make_async_remote_copy(
                src_ref=src(in_depth(r)), dst_ref=dst.at[j], send_sem=ss.at[r], recv_sem=rs.at[r],
                device_id=(i, in_depth(r)), device_id_type=MESH,
            )
            for r in DEPTH_ORDER
        ]

    def along_stream(src, dst, ss, rs):
        return [
            pltpu.make_async_remote_copy(
                src_ref=src(in_stream(r)), dst_ref=dst.at[i], send_sem=ss.at[r], recv_sem=rs.at[r],
                device_id=(in_stream(r), j), device_id_type=MESH,
            )
            for r in STREAM_ORDER
        ]

    def start(copies):
        for copy in copies:
            copy.start()

    def arrive(copies):
        for copy in copies:
            copy.wait_recv()

    def sent(copies):
        for copy in copies:
            copy.wait_send()

    def halo(n, k):
        xlow = velv.at[k, 0] if n == 0 else xs.at[n, 0, k]
        xhigh = velv.at[k, SX - 1] if n == 0 else xs.at[n, 1, k]

        def copy(src, dst, which, device):
            return pltpu.make_async_remote_copy(
                src_ref=src, dst_ref=dst, send_sem=hss.at[n, which, k], recv_sem=hrs.at[n, which, k],
                device_id=device, device_id_type=MESH,
            )

        return (
            (j < ND - 1, j > 0, copy(ds.at[n, 1, k], dr.at[n, 0, k], 2, (i, lax.rem(j + 1, ND)))),
            (j > 0, j < ND - 1, copy(ds.at[n, 0, k], dr.at[n, 1, k], 3, (i, lax.rem(j + ND - 1, ND)))),
            (i < NS - 1, i > 0, copy(xhigh, xr.at[n, 0, k], 0, (lax.rem(i + 1, NS), j))),
            (i > 0, i < NS - 1, copy(xlow, xr.at[n, 1, k], 1, (lax.rem(i + NS - 1, NS), j))),
        )

    def halo_start(n, k):
        for send, _, copy in halo(n, k):
            pl.when(send)(copy.start)

    def halo_arrive(n, k):
        for _, receive, copy in halo(n, k):
            pl.when(receive)(copy.wait_recv)

    def halo_sent(n):
        for k in range(3):
            for send, _, copy in halo(n, k):
                pl.when(send)(copy.wait_send)

    for edge, ref, side in ((i == 0, xr, 0), (i == NS - 1, xr, 1), (j == 0, dr, 0), (j == ND - 1, dr, 1)):

        @pl.when(edge)
        def _(ref=ref, side=side):
            for n in range(SWEEPS):
                ref[n, side] = jnp.zeros(ref.shape[2:], BF16)

    zero8 = jnp.zeros((8, SPAN), F32)
    for q in (qa, qb):
        for k in range(3):
            for x in (0, SX + 1):
                q[k, pl.ds(x * SLAB, SLAB), :] = jnp.zeros((SLAB, SPAN), F32)

    def clear(x, carry):
        for q in (qa, qb):
            for k in range(3):
                q[k, pl.ds(pl.multiple_of(x * SLAB, 8), 8), :] = zero8
                q[k, pl.ds(pl.multiple_of(x * SLAB + LEAD + SD, 8), 8), :] = zero8
        return carry

    lax.fori_loop(1, SX + 1, clear, 0)

    apart = (iota((SPAN, SPAN), 0) - iota((SPAN, SPAN), 1)) & (SPAN - 1)
    beside[...] = jnp.where((apart == 1) | (apart == SPAN - 1), 1.0, 0.0).astype(BF16)


    def widen(x, carry):
        at = pl.multiple_of((x + 1) * SLAB + LEAD, 8)
        for k in range(3):
            qa[k, pl.ds(at, SD), :] = velv[k, x].astype(F32)
        kappa = difv[x].astype(F32)
        speed = advv[x].astype(F32)
        rows = pl.ds(pl.multiple_of(x * SD, 8), SD)
        ka[rows, :] = kappa
        be[rows, :] = kappa + speed
        al[rows, :] = 1.0 - 6.0 * kappa - speed
        return carry

    for p, copies in enumerate(field_loads):
        for copy in copies:
            copy.wait()
        lax.fori_loop(p * (SX // PARTS), (p + 1) * (SX // PARTS), widen, 0, unroll=4)
    loads = [
        pltpu.make_async_copy(s, d, lsem.at[n])
        for n, (s, d) in enumerate(
            (
                (owner_in, owner),
                (cls_in, cls),
                (leaf_in, leaf),
                (cell_in, cell),
                (loct_in, loct),
                (noct_in, noct),
                (soct_in, soct),
                (coct_in, coct),
                (roct_in, roct),
                (nrm, nrmv),
                (exp, expv),
                (tr.at[:, pl.ds(0, SPAN)], tv.at[0, pl.ds(0, 8 * COEF), :]),
                (tr.at[:, pl.ds(SPAN, SPAN)], tv.at[1, pl.ds(0, 8 * COEF), :]),
                (tr.at[:, pl.ds(2 * SPAN, COEF - 2 * SPAN)], trv),
            )
        )
    ]
    low = pl.ds(SLAB + LEAD, SX, stride=SLAB)
    high = pl.ds(SLAB + LEAD + SD - 1, SX, stride=SLAB)
    for k in range(3):
        ds[0, 0, k] = qa[k, low, :].astype(BF16)
        ds[0, 1, k] = qa[k, high, :].astype(BF16)

    pl.semaphore_wait(barrier, ND - 1 + NS - 1)
    for k in range(3):
        halo_start(0, k)
    for copy in loads:
        copy.start()

    for copy in loads[:9]:
        copy.wait()
    own = owner[...]
    across = jnp.broadcast_to(own.astype(F32), (TILES, TILES))
    down = jnp.transpose(across)
    before = iota((TILES, TILES), 0) < iota((TILES, TILES), 1)
    rank = jnp.sum(jnp.where((across == down) & before, 1.0, 0.0), axis=0, keepdims=True).astype(I32)
    slot = (own & (ND - 1)) * (2 * NS) + (own >> 4) * 2 + rank
    pmat[...] = jnp.where(iota((SLOTS, TILES), 0) == slot, 1.0, 0.0).astype(BF16)
    feature = iota((SPAN, TILES), 0)
    meta = jnp.where((feature == leaf[...]) | (feature == cls[...] + LEAVES), 1.0, 0.0).astype(BF16)
    m1s[...] = dot_nt(pmat[...], meta).astype(BF16).reshape(ND, 2 * NS, SPAN)
    out = iota((SLOTS, SLOTS), 0)
    source = ((out >> 1) & (ND - 1)) * (2 * NS) + (out >> 5) * 2 + (out & 1)
    perm[...] = jnp.where(iota((SLOTS, SLOTS), 1) == source, 1.0, 0.0).astype(BF16)

    meta1 = along_depth(lambda p: m1s.at[p], m1r, m1ss, m1rs)
    start(meta1)
    m1r[j] = m1s[j]

    def sweep(src, dst, pitch, lead):
        slabs = src.reshape(3, SX + 2, SLAB, SPAN)

        def step(x, carry):
            rows = pl.ds(pl.multiple_of(x * SD, 8), SD)
            kappa, beta, alpha = ka[rows, :], be[rows, :], al[rows, :]
            for k in range(3):
                c = slabs[k, x + 1, pl.ds(LEAD, SD), :]
                f = slabs[k, x + 2, pl.ds(LEAD, SD), :]
                b = slabs[k, x, pl.ds(LEAD, SD), :]
                up = slabs[k, x + 1, pl.ds(LEAD + 1, SD), :]
                down = slabs[k, x + 1, pl.ds(LEAD - 1, SD), :]
                total = f + (up + down) + dot(c.astype(BF16), beside[...])
                dst[k, pl.ds(pl.multiple_of(x * pitch + lead, 8), SD), :] = alpha * c + kappa * total + beta * b
            return carry

        lax.fori_loop(0, SX, step, 0, unroll=UNROLL)

    def faces(n, dst, pitch, lead):
        first = pl.ds(lead, SD)
        last = pl.ds((SX - 1) * pitch + lead, SD)
        low = pl.ds(lead, SX, stride=pitch)
        high = pl.ds(lead + SD - 1, SX, stride=pitch)
        klow = ka[pl.ds(0, SX, stride=SD), :]
        khigh = ka[pl.ds(SD - 1, SX, stride=SD), :]
        for k in range(3):
            halo_arrive(n, k)
            qf = dst[k, first, :] + be[pl.ds(0, SD), :] * xr[n, 0, k].astype(F32)
            ql = dst[k, last, :] + ka[pl.ds((SX - 1) * SD, SD), :] * xr[n, 1, k].astype(F32)
            dst[k, first, :] = qf
            dst[k, last, :] = ql
            ql = dst[k, low, :] + klow * dr[n, 0, k].astype(F32)
            qh = dst[k, high, :] + khigh * dr[n, 1, k].astype(F32)
            dst[k, low, :] = ql
            dst[k, high, :] = qh
            if n + 1 < SWEEPS:
                ds[n + 1, 0, k] = ql.astype(BF16)
                ds[n + 1, 1, k] = qh.astype(BF16)
                xs[n + 1, 0, k] = dst[k, first, :].astype(BF16)
                xs[n + 1, 1, k] = dst[k, last, :].astype(BF16)
                halo_start(n + 1, k)

    sweep(qa, qb, SLAB, SLAB + LEAD)
    faces(0, qb, SLAB, SLAB + LEAD)

    sweep(qb, qa, SLAB, SLAB + LEAD)
    arrive(meta1)
    m2s[...] = dot(perm[...], m1r[...].reshape(SLOTS, SPAN)).astype(BF16).reshape(NS, 2 * ND, SPAN)
    meta2 = along_stream(lambda p: m2s.at[p], m2r, m2ss, m2rs)
    start(meta2)
    m2r[i] = m2s[i]
    faces(1, qa, SLAB, SLAB + LEAD)

    sweep(qa, qb, SLAB, SLAB + LEAD)
    faces(2, qb, SLAB, SLAB + LEAD)

    sweep(qb, flow, SD, 0)
    faces(3, flow, SD, 0)

    loads[9].wait()

    def sample(t, carry):
        for k in range(3):
            picked[k, t] = flow[k, cell[0, t]]
        return carry

    lax.fori_loop(0, TILES, sample, 0, unroll=8)
    strength = nrmv[0].astype(F32) * picked[0]
    for k in (1, 2):
        strength = strength + nrmv[k].astype(F32) * picked[k]
    a1s[...] = dot(pmat[...], strength.astype(BF16)).astype(BF16).reshape(ND, 2 * NS, SPAN)
    data1 = along_depth(lambda p: a1s.at[p], a1r, a1ss, a1rs)
    start(data1)
    a1r[j] = a1s[j]

    loads[10].wait()
    ef[pl.ds(0, 8 * COEF), :] = expv[...].astype(F32)
    ef[pl.ds(8 * COEF, 8 * (KP - COEF)), :] = jnp.zeros((8 * (KP - COEF), SPAN), F32)

    def classes(c, carry):
        for n in range(3):
            value = jnp.transpose(ef[pl.ds(8 * SPAN * n + c, SPAN, stride=8), :])
            et[pl.ds(pl.multiple_of(c * SPAN, SPAN), SPAN), pl.ds(n * SPAN, SPAN)] = value.astype(BF16)
        return carry

    lax.fori_loop(0, 8, classes, 0)
    for copy in loads[11:]:
        copy.wait()
    for o in range(8):
        w[o, pl.ds(KR, KP - KR), :] = jnp.zeros((KP - KR, 2 * KP), BF16)
    tv[:, pl.ds(8 * COEF, 8 * (KR - COEF)), :] = jnp.zeros((3, 8 * (KR - COEF), SPAN), F32)
    tv[2, pl.ds(0, 8 * COEF), :] = jnp.concatenate(
        [trv[...], jnp.zeros((8 * COEF, KP - COEF), F32)], axis=1
    )

    def halve(b, carry):
        for o in range(8):
            rows = pl.ds(b * 128 + o, 16, stride=8)
            to = pl.ds(pl.multiple_of(b * 16, 16), 16)
            for n in range(3):
                lanes = pl.ds(n * SPAN, SPAN)
                h, l = split(tv[n, rows, :])
                w[o, to, lanes] = h.astype(BF16)
                w[o, to, pl.ds(KP + n * SPAN, SPAN)] = l.astype(BF16)
        return carry

    lax.fori_loop(0, KR // 16, halve, 0)
    arrive(meta2)
    lane = iota((1, SPAN), 1)
    octant = jnp.full((1, SPAN), -1, I32)
    for l in range(LEAVES):
        octant = jnp.where(lane == l, loct[l // 8, l % 8], octant)
    row = iota((SPAN, SPAN), 0)
    ordered = jnp.where((row & 7) == (lane >> 3), jnp.where((row >> 3) == octant, 1.0, 0.0), 0.0)
    order[...] = jnp.transpose(ordered).astype(BF16)
    arrived = m2r[...].reshape(SLOTS, SPAN)
    leaf_of = dot_nt(ordered[:LEAVES].astype(BF16), arrived)
    pick = jnp.where(iota((8, SPAN), 1) == iota((8, SPAN), 0) + LEAVES, 1.0, 0.0).astype(BF16)
    class_of = dot_nt(pick, arrived)
    for c in range(8):
        gg[pl.ds(c * LEAVES, LEAVES), :] = (leaf_of * class_of[c : c + 1, :]).astype(BF16)
    arrive(data1)
    a2s[...] = dot(perm[...], a1r[...].reshape(SLOTS, SPAN)).astype(BF16).reshape(NS, 2 * ND, SPAN)
    data2 = along_stream(lambda p: a2s.at[p], a2r, a2ss, a2rs)
    start(data2)
    a2r[i] = a2s[i]

    group, member = lax.div(j, 8), lax.rem(j, 8)
    table = soct[group, member]
    high, low = w[table][:, :KP], w[table][:, KP:]
    lifts[:, :KP] = high
    lifts[:, pl.ds(3 * KP, KP)] = low
    for n, table in ((1, coct[group, i]), (2, roct[0, group])):
        following = w[table]
        h, l = split(dot(high, following[:, :KP]) + dot(low, following[:, :KP]) + dot(high, following[:, KP:]))
        high, low = h.astype(BF16), l.astype(BF16)
        lifts[:, pl.ds(n * KP, KP)] = high
        lifts[:, pl.ds((3 + n) * KP, KP)] = low
    arrive(data2)

    sums = dot(gg[...], a2r[...].reshape(SLOTS, SPAN))
    blocks = []
    for c in range(8):
        h, l = split(sums[c * LEAVES : (c + 1) * LEAVES])
        blocks.append(jnp.concatenate([h, l], axis=0).astype(BF16))
    both = dot(jnp.concatenate(blocks, axis=1), et[...])
    ordered_leaves = both[:LEAVES] + both[LEAVES:]

    h, l = split(ordered_leaves)
    lhs = jnp.concatenate(
        [jnp.concatenate([h[8 * o : 8 * o + 8], l[8 * o : 8 * o + 8]], axis=0).astype(BF16) for o in range(8)], axis=1
    )
    product = dot(lhs, w[...].reshape(8 * KP, 2 * KP))
    product = product[:8] + product[8:]
    h, l = split(product[:, :KP] + product[:, KP:])
    node = iota((16, KP), 0) & 7
    octant = jnp.full((16, KP), -1, I32)
    for p in range(8):
        octant = jnp.where(node == p, noct[0, p], octant)
    stacked = jnp.concatenate([h, l], axis=0)
    lhs = jnp.concatenate([jnp.where(octant == o, stacked, 0.0).astype(BF16) for o in range(8)], axis=1)
    product = dot(lhs, w[...].reshape(8 * KP, 2 * KP))
    subtree = jnp.sum(product[:, :KP] + product[:, KP:], axis=0, keepdims=True)

    h, l = split(subtree)
    place = iota((16, KP), 0)
    lhs = jnp.where(place == 0, h, jnp.where(place == 1, l, 0.0)).astype(BF16)
    product = dot(lhs, lifts[...])
    e1s[...] = jnp.sum(product[:, : 3 * KP] + product[:, 3 * KP :], axis=0, keepdims=True)
    terms = along_depth(lambda p: e1s, e1r, e1ss, e1rs)
    start(terms)
    e1r[j] = e1s[...]

    h, rest = split(ordered_leaves)
    m, l = split(rest)
    turn = order[:LEAVES, :LEAVES]
    leaves[...] = (dot(turn, h.astype(BF16)) + dot(turn, m.astype(BF16)) + dot(turn, l.astype(BF16)))[:, :COEF]

    arrive(terms)
    halves = []
    for g in range(2):
        total = e1r[8 * g]
        for m in range(1, 8):
            total = total + e1r[8 * g + m]
        halves.append(total)
    e2s[...] = jnp.concatenate(
        [
            halves[0][:, :KP],
            halves[1][:, :KP],
            halves[0][:, KP : 2 * KP],
            halves[1][:, KP : 2 * KP],
            halves[0][:, 2 * KP :] + halves[1][:, 2 * KP :],
        ],
        axis=1,
    )
    rows = along_stream(lambda p: e2s, e2r, e2ss, e2rs)
    start(rows)
    e2r[i] = e2s[...]
    arrive(rows)
    total = e2r[0][:, 2 * KP :]
    for s in range(1, NS):
        total = total + e2r[s][:, 2 * KP :]
    for s in range(NS):
        value = e2r[s]
        for g in range(2):
            upper[pl.ds(2 * s + g, 1), :] = value[:, g * KP : g * KP + COEF]
    for n in range(3):
        upper[pl.ds(2 * NS + n, 1), :] = total[:, n * KP : n * KP + COEF]

    for n in range(SWEEPS):
        halo_sent(n)
    for copies in (meta1, meta2, data1, data2, terms, rows):
        sent(copies)


def write_out(*refs):
    copies = [pltpu.make_async_copy(refs[n], refs[n + 3], refs[6].at[n]) for n in range(3)]
    for copy in copies:
        copy.start()
    for copy in copies:
        copy.wait()


def per_device(
    velocity, diffusion, advection, normals, tile_cell, tile_class, tile_leaf, tile_owner,
    source_expansion, translation, leaf_octant, node_octant, subtree_octant, cluster_octant, root_octant,
):
    vmem = pl.BlockSpec(memory_space=pltpu.VMEM)
    hbm = pl.BlockSpec(memory_space=pltpu.HBM)
    dma = pltpu.SemaphoreType.DMA
    rows = (SX + 2) * SLAB
    shapes = ((3, SX * SD, SPAN), (LEAVES, COEF), (2 * NS + 3, COEF))
    results = pl.pallas_call(
        kernel,
        out_shape=tuple(pltpu.VMEM(shape, F32) for shape in shapes),
        in_specs=[hbm] * 15,
        out_specs=(vmem, vmem, vmem),
        scratch_shapes=[
            pltpu.SMEM((1, TILES), I32),
            pltpu.SMEM((8, 8), I32),
            pltpu.SMEM((1, 8), I32),
            pltpu.SMEM((2, 8), I32),
            pltpu.SMEM((2, 8), I32),
            pltpu.SMEM((1, 8), I32),
            pltpu.VMEM((1, TILES), I32),
            pltpu.VMEM((1, TILES), I32),
            pltpu.VMEM((1, TILES), I32),
            pltpu.VMEM((3, SX, SD, SPAN), BF16),
            pltpu.VMEM((SX, SD, SPAN), BF16),
            pltpu.VMEM((SX, SD, SPAN), BF16),
            pltpu.VMEM((3, TILES, SPAN), BF16),
            pltpu.VMEM((8 * COEF, SPAN), BF16),
            pltpu.VMEM((8 * COEF, COEF - 2 * SPAN), F32),
            pltpu.VMEM((3, 8 * KR, SPAN), F32),
            pltpu.VMEM((8 * KP, SPAN), F32),
            pltpu.VMEM((8 * SPAN, KP), BF16),
            pltpu.VMEM((8, KP, 2 * KP), BF16),
            pltpu.VMEM((3, rows, SPAN), F32),
            pltpu.VMEM((3, rows, SPAN), F32),
            pltpu.VMEM((SX * SD, SPAN), F32),
            pltpu.VMEM((SX * SD, SPAN), F32),
            pltpu.VMEM((SX * SD, SPAN), F32),
            pltpu.VMEM((SLOTS, TILES), BF16),
            pltpu.VMEM((SLOTS, SLOTS), BF16),
            pltpu.VMEM((8 * LEAVES, SLOTS), BF16),
            pltpu.VMEM((3, TILES, SPAN), F32),
            pltpu.VMEM((SPAN, SPAN), BF16),
            pltpu.VMEM((SPAN, SPAN), BF16),
            pltpu.VMEM((KP, 6 * KP), BF16),
            pltpu.VMEM((SWEEPS, 2, 3, SD, SPAN), BF16),
            pltpu.VMEM((SWEEPS, 2, 3, SD, SPAN), BF16),
            pltpu.VMEM((SWEEPS, 2, 3, SX, SPAN), BF16),
            pltpu.VMEM((SWEEPS, 2, 3, SX, SPAN), BF16),
            pltpu.VMEM((ND, 2 * NS, SPAN), BF16),
            pltpu.VMEM((ND, 2 * NS, SPAN), BF16),
            pltpu.VMEM((NS, 2 * ND, SPAN), BF16),
            pltpu.VMEM((NS, 2 * ND, SPAN), BF16),
            pltpu.VMEM((ND, 2 * NS, SPAN), BF16),
            pltpu.VMEM((ND, 2 * NS, SPAN), BF16),
            pltpu.VMEM((NS, 2 * ND, SPAN), BF16),
            pltpu.VMEM((NS, 2 * ND, SPAN), BF16),
            pltpu.VMEM((1, 3 * KP), F32),
            pltpu.VMEM((ND, 1, 3 * KP), F32),
            pltpu.VMEM((1, 5 * KP), F32),
            pltpu.VMEM((NS, 1, 5 * KP), F32),
            dma((3, PARTS)),
            dma((14,)),
            dma((SWEEPS, 4, 3)),
            dma((SWEEPS, 4, 3)),
            dma((ND,)), dma((ND,)), dma((NS,)), dma((NS,)),
            dma((ND,)), dma((ND,)), dma((NS,)), dma((NS,)),
            dma((ND,)), dma((ND,)), dma((NS,)), dma((NS,)),
        ],
        compiler_params=pltpu.CompilerParams(
            collective_id=0, has_side_effects=True, vmem_limit_bytes=60400 * 1024
        ),
        cost_estimate=pl.CostEstimate(flops=10**8, bytes_accessed=12 * 10**6, transcendentals=0),
    )(
        tile_cell.reshape(1, TILES),
        leaf_octant.reshape(8, 8),
        node_octant.reshape(1, 8),
        subtree_octant.reshape(2, 8),
        cluster_octant,
        root_octant.reshape(1, 8),
        tile_owner.reshape(1, TILES),
        tile_class.reshape(1, TILES),
        tile_leaf.reshape(1, TILES),
        velocity,
        diffusion,
        advection,
        normals.reshape(3, TILES, SPAN),
        jnp.transpose(source_expansion, (2, 0, 1)).reshape(8 * COEF, SPAN),
        jnp.transpose(translation, (1, 0, 2)).reshape(8 * COEF, COEF),
    )
    flow, leaves, upper = pl.pallas_call(
        write_out,
        out_shape=tuple(jax.ShapeDtypeStruct(shape, F32) for shape in shapes),
        in_specs=[vmem] * 3,
        out_specs=[hbm] * 3,
        scratch_shapes=[dma((3,))],
        compiler_params=pltpu.CompilerParams(vmem_limit_bytes=1024 * 1024),
    )(*results)
    return flow.reshape(3, SX, SD, SPAN), leaves.reshape(1, 1, LEAVES, COEF), upper


def solution(mesh):
    in_specs = (
        P(None, "stream", "depth", None),
        P("stream", "depth", None),
        P("stream", "depth", None),
        P("stream", "depth", None, None, None),
        P("stream", "depth", None),
        P("stream", "depth", None),
        P("stream", "depth", None),
        P("stream", "depth", None, None),
        P(),
        P(),
        P("stream", "depth", None, None),
        P("stream", "depth", None),
        P("stream", None, None),
        P(),
        P(),
    )
    out_specs = (P(None, "stream", "depth", None), P("stream", "depth", None, None), P())
    return jax.shard_map(
        per_device, mesh=mesh, in_specs=in_specs, out_specs=out_specs, check_vma=False
    )
```

```python
import functools

import jax
import jax.numpy as jnp
from jax import lax
from jax.experimental import pallas as pl
from jax.experimental.pallas import tpu as pltpu
from jax.sharding import PartitionSpec as P

MESH = pl.DeviceIdType.MESH
F32, BF16, I32 = jnp.float32, jnp.bfloat16, jnp.int32
SX, SD, SPAN, SWEEPS, TILES, COEF, LEAVES = 64, 48, 128, 4, 128, 289, 64
NS, ND = 8, 16
SLAB, LEAD = 64, 8
KP = 384
KR = 304
SLOTS = 2 * NS * ND
UNROLL = 16
PARTS = 2


def split(value):
    high = value.astype(BF16).astype(F32)
    return high, value - high


def dot(a, b):
    return jnp.dot(a, b, preferred_element_type=F32)


def dot_nt(a, b):
    return lax.dot_general(a, b, (((1,), (1,)), ((), ())), preferred_element_type=F32)


DEPTH_ORDER = (10, 9, 11, 6, 14, 5, 7, 13, 15, 8, 2, 4, 12, 1, 3)
STREAM_ORDER = (5, 4, 3, 7, 2, 6, 1)


def flip(value, bits):
    if bits == 0:
        return value
    if bits == 1:
        return value + 1 - 2 * lax.rem(value, 2)
    if bits == 2:
        return lax.rem(value + 2, 4)
    return 3 - value


def iota(shape, dim):
    return lax.broadcasted_iota(I32, shape, dim)


def kernel(
    cell_in, loct_in, noct_in, soct_in, coct_in, roct_in, owner_in, cls_in, leaf_in,
    vel, dif, adv, nrm, exp, tr,
    flow, leaves, upper,
    cell, loct, noct, soct, coct, roct, owner, cls, leaf,
    velv, difv, advv, nrmv, expv, trv, tv, ef, et, w, qa, qb, al, ka, be,
    pmat, perm, gg, picked, order, beside, lifts,
    xs, xr, ds, dr, m1s, m1r, m2s, m2r, a1s, a1r, a2s, a2r, e1s, e1r, e2s, e2r,
    fsem, lsem, hss, hrs, m1ss, m1rs, m2ss, m2rs, a1ss, a1rs, a2ss, a2rs, e1ss, e1rs, e2ss, e2rs,
):
    i, j = lax.axis_index("stream"), lax.axis_index("depth")

    def in_depth(r):
        return 4 * flip(lax.div(j, 4), r // 4) + flip(lax.rem(j, 4), r % 4)

    def in_stream(r):
        core = lax.rem(i, 2)
        return 2 * flip(lax.div(i, 2), r // 2) + (1 - core if r % 2 else core)

    barrier = pltpu.get_barrier_semaphore()
    for r in DEPTH_ORDER:
        pl.semaphore_signal(barrier, inc=1, device_id=(i, in_depth(r)), device_id_type=MESH)
    for r in STREAM_ORDER:
        pl.semaphore_signal(barrier, inc=1, device_id=(in_stream(r), j), device_id_type=MESH)

    def part(src, dst, n, p):
        rows = pl.ds(p * (SX // PARTS), SX // PARTS)
        at = (slice(None), rows) if len(src.shape) == 4 else (rows,)
        return pltpu.make_async_copy(src.at[at], dst.at[at], fsem.at[n, p])

    field_loads = [
        [part(s, d, n, p) for n, (s, d) in enumerate(((vel, velv), (dif, difv), (adv, advv)))] for p in range(PARTS)
    ]
    for copies in field_loads:
        for copy in copies:
            copy.start()

    def along_depth(src, dst, ss, rs):
        return [
            pltpu.make_async_remote_copy(
                src_ref=src(in_depth(r)), dst_ref=dst.at[j], send_sem=ss.at[r], recv_sem=rs.at[r],
                device_id=(i, in_depth(r)), device_id_type=MESH,
            )
            for r in DEPTH_ORDER
        ]

    def along_stream(src, dst, ss, rs):
        return [
            pltpu.make_async_remote_copy(
                src_ref=src(in_stream(r)), dst_ref=dst.at[i], send_sem=ss.at[r], recv_sem=rs.at[r],
                device_id=(in_stream(r), j), device_id_type=MESH,
            )
            for r in STREAM_ORDER
        ]

    def start(copies):
        for copy in copies:
            copy.start()

    def arrive(copies):
        for copy in copies:
            copy.wait_recv()

    def sent(copies):
        for copy in copies:
            copy.wait_send()

    def halo(n, k):
        xlow = velv.at[k, 0] if n == 0 else xs.at[n, 0, k]
        xhigh = velv.at[k, SX - 1] if n == 0 else xs.at[n, 1, k]

        def copy(src, dst, which, device):
            return pltpu.make_async_remote_copy(
                src_ref=src, dst_ref=dst, send_sem=hss.at[n, which, k], recv_sem=hrs.at[n, which, k],
                device_id=device, device_id_type=MESH,
            )

        return (
            (j < ND - 1, j > 0, copy(ds.at[n, 1, k], dr.at[n, 0, k], 2, (i, lax.rem(j + 1, ND)))),
            (j > 0, j < ND - 1, copy(ds.at[n, 0, k], dr.at[n, 1, k], 3, (i, lax.rem(j + ND - 1, ND)))),
            (i < NS - 1, i > 0, copy(xhigh, xr.at[n, 0, k], 0, (lax.rem(i + 1, NS), j))),
            (i > 0, i < NS - 1, copy(xlow, xr.at[n, 1, k], 1, (lax.rem(i + NS - 1, NS), j))),
        )

    def halo_start(n, k):
        for send, _, copy in halo(n, k):
            pl.when(send)(copy.start)

    def halo_arrive(n, k):
        for _, receive, copy in halo(n, k):
            pl.when(receive)(copy.wait_recv)

    def halo_sent(n):
        for k in range(3):
            for send, _, copy in halo(n, k):
                pl.when(send)(copy.wait_send)

    for edge, ref, side in ((i == 0, xr, 0), (i == NS - 1, xr, 1), (j == 0, dr, 0), (j == ND - 1, dr, 1)):

        @pl.when(edge)
        def _(ref=ref, side=side):
            for n in range(SWEEPS):
                ref[n, side] = jnp.zeros(ref.shape[2:], BF16)

    zero8 = jnp.zeros((8, SPAN), F32)
    for q in (qa, qb):
        for k in range(3):
            for x in (0, SX + 1):
                q[k, pl.ds(x * SLAB, SLAB), :] = jnp.zeros((SLAB, SPAN), F32)

    def clear(x, carry):
        for q in (qa, qb):
            for k in range(3):
                q[k, pl.ds(pl.multiple_of(x * SLAB, 8), 8), :] = zero8
                q[k, pl.ds(pl.multiple_of(x * SLAB + LEAD + SD, 8), 8), :] = zero8
        return carry

    lax.fori_loop(1, SX + 1, clear, 0)

    apart = (iota((SPAN, SPAN), 0) - iota((SPAN, SPAN), 1)) & (SPAN - 1)
    beside[...] = jnp.where((apart == 1) | (apart == SPAN - 1), 1.0, 0.0).astype(BF16)


    def widen(x, carry):
        at = pl.multiple_of((x + 1) * SLAB + LEAD, 8)
        for k in range(3):
            qa[k, pl.ds(at, SD), :] = velv[k, x].astype(F32)
        kappa = difv[x].astype(F32)
        speed = advv[x].astype(F32)
        rows = pl.ds(pl.multiple_of(x * SD, 8), SD)
        ka[rows, :] = kappa
        be[rows, :] = kappa + speed
        al[rows, :] = 1.0 - 6.0 * kappa - speed
        return carry

    for p, copies in enumerate(field_loads):
        for copy in copies:
            copy.wait()
        lax.fori_loop(p * (SX // PARTS), (p + 1) * (SX // PARTS), widen, 0, unroll=4)
    loads = [
        pltpu.make_async_copy(s, d, lsem.at[n])
        for n, (s, d) in enumerate(
            (
                (owner_in, owner),
                (cls_in, cls),
                (leaf_in, leaf),
                (cell_in, cell),
                (loct_in, loct),
                (noct_in, noct),
                (soct_in, soct),
                (coct_in, coct),
                (roct_in, roct),
                (nrm, nrmv),
                (exp, expv),
                (tr.at[:, pl.ds(0, SPAN)], tv.at[0, pl.ds(0, 8 * COEF), :]),
                (tr.at[:, pl.ds(SPAN, SPAN)], tv.at[1, pl.ds(0, 8 * COEF), :]),
                (tr.at[:, pl.ds(2 * SPAN, COEF - 2 * SPAN)], trv),
            )
        )
    ]
    low = pl.ds(SLAB + LEAD, SX, stride=SLAB)
    high = pl.ds(SLAB + LEAD + SD - 1, SX, stride=SLAB)
    for k in range(3):
        ds[0, 0, k] = qa[k, low, :].astype(BF16)
        ds[0, 1, k] = qa[k, high, :].astype(BF16)

    pl.semaphore_wait(barrier, ND - 1 + NS - 1)
    for k in range(3):
        halo_start(0, k)
    for copy in loads:
        copy.start()

    for copy in loads[:9]:
        copy.wait()
    own = owner[...]
    across = jnp.broadcast_to(own.astype(F32), (TILES, TILES))
    down = jnp.transpose(across)
    before = iota((TILES, TILES), 0) < iota((TILES, TILES), 1)
    rank = jnp.sum(jnp.where((across == down) & before, 1.0, 0.0), axis=0, keepdims=True).astype(I32)
    slot = (own & (ND - 1)) * (2 * NS) + (own >> 4) * 2 + rank
    pmat[...] = jnp.where(iota((SLOTS, TILES), 0) == slot, 1.0, 0.0).astype(BF16)
    feature = iota((SPAN, TILES), 0)
    meta = jnp.where((feature == leaf[...]) | (feature == cls[...] + LEAVES), 1.0, 0.0).astype(BF16)
    m1s[...] = dot_nt(pmat[...], meta).astype(BF16).reshape(ND, 2 * NS, SPAN)
    out = iota((SLOTS, SLOTS), 0)
    source = ((out >> 1) & (ND - 1)) * (2 * NS) + (out >> 5) * 2 + (out & 1)
    perm[...] = jnp.where(iota((SLOTS, SLOTS), 1) == source, 1.0, 0.0).astype(BF16)

    meta1 = along_depth(lambda p: m1s.at[p], m1r, m1ss, m1rs)
    start(meta1)
    m1r[j] = m1s[j]

    def sweep(src, dst, pitch, lead):
        slabs = src.reshape(3, SX + 2, SLAB, SPAN)

        def step(x, carry):
            rows = pl.ds(pl.multiple_of(x * SD, 8), SD)
            kappa, beta, alpha = ka[rows, :], be[rows, :], al[rows, :]
            for k in range(3):
                c = slabs[k, x + 1, pl.ds(LEAD, SD), :]
                f = slabs[k, x + 2, pl.ds(LEAD, SD), :]
                b = slabs[k, x, pl.ds(LEAD, SD), :]
                up = slabs[k, x + 1, pl.ds(LEAD + 1, SD), :]
                down = slabs[k, x + 1, pl.ds(LEAD - 1, SD), :]
                total = f + (up + down) + dot(c.astype(BF16), beside[...])
                dst[k, pl.ds(pl.multiple_of(x * pitch + lead, 8), SD), :] = alpha * c + kappa * total + beta * b
            return carry

        lax.fori_loop(0, SX, step, 0, unroll=UNROLL)

    def faces(n, dst, pitch, lead):
        first = pl.ds(lead, SD)
        last = pl.ds((SX - 1) * pitch + lead, SD)
        low = pl.ds(lead, SX, stride=pitch)
        high = pl.ds(lead + SD - 1, SX, stride=pitch)
        klow = ka[pl.ds(0, SX, stride=SD), :]
        khigh = ka[pl.ds(SD - 1, SX, stride=SD), :]
        for k in range(3):
            halo_arrive(n, k)
            qf = dst[k, first, :] + be[pl.ds(0, SD), :] * xr[n, 0, k].astype(F32)
            ql = dst[k, last, :] + ka[pl.ds((SX - 1) * SD, SD), :] * xr[n, 1, k].astype(F32)
            dst[k, first, :] = qf
            dst[k, last, :] = ql
            ql = dst[k, low, :] + klow * dr[n, 0, k].astype(F32)
            qh = dst[k, high, :] + khigh * dr[n, 1, k].astype(F32)
            dst[k, low, :] = ql
            dst[k, high, :] = qh
            if n + 1 < SWEEPS:
                ds[n + 1, 0, k] = ql.astype(BF16)
                ds[n + 1, 1, k] = qh.astype(BF16)
                xs[n + 1, 0, k] = dst[k, first, :].astype(BF16)
                xs[n + 1, 1, k] = dst[k, last, :].astype(BF16)
                halo_start(n + 1, k)

    sweep(qa, qb, SLAB, SLAB + LEAD)
    faces(0, qb, SLAB, SLAB + LEAD)

    sweep(qb, qa, SLAB, SLAB + LEAD)
    arrive(meta1)
    m2s[...] = dot(perm[...], m1r[...].reshape(SLOTS, SPAN)).astype(BF16).reshape(NS, 2 * ND, SPAN)
    meta2 = along_stream(lambda p: m2s.at[p], m2r, m2ss, m2rs)
    start(meta2)
    m2r[i] = m2s[i]
    faces(1, qa, SLAB, SLAB + LEAD)

    sweep(qa, qb, SLAB, SLAB + LEAD)
    faces(2, qb, SLAB, SLAB + LEAD)

    sweep(qb, flow, SD, 0)
    faces(3, flow, SD, 0)

    loads[9].wait()

    def sample(t, carry):
        for k in range(3):
            picked[k, t] = flow[k, cell[0, t]]
        return carry

    lax.fori_loop(0, TILES, sample, 0, unroll=8)
    strength = nrmv[0].astype(F32) * picked[0]
    for k in (1, 2):
        strength = strength + nrmv[k].astype(F32) * picked[k]
    a1s[...] = dot(pmat[...], strength.astype(BF16)).astype(BF16).reshape(ND, 2 * NS, SPAN)
    data1 = along_depth(lambda p: a1s.at[p], a1r, a1ss, a1rs)
    start(data1)
    a1r[j] = a1s[j]

    loads[10].wait()
    ef[pl.ds(0, 8 * COEF), :] = expv[...].astype(F32)
    ef[pl.ds(8 * COEF, 8 * (KP - COEF)), :] = jnp.zeros((8 * (KP - COEF), SPAN), F32)

    def classes(c, carry):
        for n in range(3):
            value = jnp.transpose(ef[pl.ds(8 * SPAN * n + c, SPAN, stride=8), :])
            et[pl.ds(pl.multiple_of(c * SPAN, SPAN), SPAN), pl.ds(n * SPAN, SPAN)] = value.astype(BF16)
        return carry

    lax.fori_loop(0, 8, classes, 0)
    for copy in loads[11:]:
        copy.wait()
    for o in range(8):
        w[o, pl.ds(KR, KP - KR), :] = jnp.zeros((KP - KR, 2 * KP), BF16)
    tv[:, pl.ds(8 * COEF, 8 * (KR - COEF)), :] = jnp.zeros((3, 8 * (KR - COEF), SPAN), F32)
    tv[2, pl.ds(0, 8 * COEF), :] = jnp.concatenate(
        [trv[...], jnp.zeros((8 * COEF, KP - COEF), F32)], axis=1
    )

    def halve(b, carry):
        for o in range(8):
            rows = pl.ds(b * 128 + o, 16, stride=8)
            to = pl.ds(pl.multiple_of(b * 16, 16), 16)
            for n in range(3):
                lanes = pl.ds(n * SPAN, SPAN)
                h, l = split(tv[n, rows, :])
                w[o, to, lanes] = h.astype(BF16)
                w[o, to, pl.ds(KP + n * SPAN, SPAN)] = l.astype(BF16)
        return carry

    lax.fori_loop(0, KR // 16, halve, 0)
    arrive(meta2)
    lane = iota((1, SPAN), 1)
    octant = jnp.full((1, SPAN), -1, I32)
    for l in range(LEAVES):
        octant = jnp.where(lane == l, loct[l // 8, l % 8], octant)
    row = iota((SPAN, SPAN), 0)
    ordered = jnp.where((row & 7) == (lane >> 3), jnp.where((row >> 3) == octant, 1.0, 0.0), 0.0)
    order[...] = jnp.transpose(ordered).astype(BF16)
    arrived = m2r[...].reshape(SLOTS, SPAN)
    leaf_of = dot_nt(ordered[:LEAVES].astype(BF16), arrived)
    pick = jnp.where(iota((8, SPAN), 1) == iota((8, SPAN), 0) + LEAVES, 1.0, 0.0).astype(BF16)
    class_of = dot_nt(pick, arrived)
    for c in range(8):
        gg[pl.ds(c * LEAVES, LEAVES), :] = (leaf_of * class_of[c : c + 1, :]).astype(BF16)
    arrive(data1)
    a2s[...] = dot(perm[...], a1r[...].reshape(SLOTS, SPAN)).astype(BF16).reshape(NS, 2 * ND, SPAN)
    data2 = along_stream(lambda p: a2s.at[p], a2r, a2ss, a2rs)
    start(data2)
    a2r[i] = a2s[i]

    group, member = lax.div(j, 8), lax.rem(j, 8)
    table = soct[group, member]
    high, low = w[table][:, :KP], w[table][:, KP:]
    lifts[:, :KP] = high
    lifts[:, pl.ds(3 * KP, KP)] = low
    for n, table in ((1, coct[group, i]), (2, roct[0, group])):
        following = w[table]
        h, l = split(dot(high, following[:, :KP]) + dot(low, following[:, :KP]) + dot(high, following[:, KP:]))
        high, low = h.astype(BF16), l.astype(BF16)
        lifts[:, pl.ds(n * KP, KP)] = high
        lifts[:, pl.ds((3 + n) * KP, KP)] = low
    arrive(data2)

    sums = dot(gg[...], a2r[...].reshape(SLOTS, SPAN))
    blocks = []
    for c in range(8):
        h, l = split(sums[c * LEAVES : (c + 1) * LEAVES])
        blocks.append(jnp.concatenate([h, l], axis=0).astype(BF16))
    both = dot(jnp.concatenate(blocks, axis=1), et[...])
    ordered_leaves = both[:LEAVES] + both[LEAVES:]

    h, l = split(ordered_leaves)
    lhs = jnp.concatenate(
        [jnp.concatenate([h[8 * o : 8 * o + 8], l[8 * o : 8 * o + 8]], axis=0).astype(BF16) for o in range(8)], axis=1
    )
    product = dot(lhs, w[...].reshape(8 * KP, 2 * KP))
    product = product[:8] + product[8:]
    h, l = split(product[:, :KP] + product[:, KP:])
    node = iota((16, KP), 0) & 7
    octant = jnp.full((16, KP), -1, I32)
    for p in range(8):
        octant = jnp.where(node == p, noct[0, p], octant)
    stacked = jnp.concatenate([h, l], axis=0)
    lhs = jnp.concatenate([jnp.where(octant == o, stacked, 0.0).astype(BF16) for o in range(8)], axis=1)
    product = dot(lhs, w[...].reshape(8 * KP, 2 * KP))
    subtree = jnp.sum(product[:, :KP] + product[:, KP:], axis=0, keepdims=True)

    h, l = split(subtree)
    place = iota((16, KP), 0)
    lhs = jnp.where(place == 0, h, jnp.where(place == 1, l, 0.0)).astype(BF16)
    product = dot(lhs, lifts[...])
    e1s[...] = jnp.sum(product[:, : 3 * KP] + product[:, 3 * KP :], axis=0, keepdims=True)
    terms = along_depth(lambda p: e1s, e1r, e1ss, e1rs)
    start(terms)
    e1r[j] = e1s[...]

    h, rest = split(ordered_leaves)
    m, l = split(rest)
    turn = order[:LEAVES, :LEAVES]
    leaves[...] = (dot(turn, h.astype(BF16)) + dot(turn, m.astype(BF16)) + dot(turn, l.astype(BF16)))[:, :COEF]

    for n in range(SWEEPS):
        halo_sent(n)
    for copies in (meta1, meta2, data1, data2):
        sent(copies)
    arrive(terms)
    halves = []
    for g in range(2):
        total = e1r[8 * g]
        for m in range(1, 8):
            total = total + e1r[8 * g + m]
        halves.append(total)
    e2s[...] = jnp.concatenate(
        [
            halves[0][:, :KP],
            halves[1][:, :KP],
            halves[0][:, KP : 2 * KP],
            halves[1][:, KP : 2 * KP],
            halves[0][:, 2 * KP :] + halves[1][:, 2 * KP :],
        ],
        axis=1,
    )
    rows = along_stream(lambda p: e2s, e2r, e2ss, e2rs)
    start(rows)
    e2r[i] = e2s[...]
    sent(terms)
    arrive(rows)
    total = e2r[0][:, 2 * KP :]
    for s in range(1, NS):
        total = total + e2r[s][:, 2 * KP :]
    for s in range(NS):
        value = e2r[s]
        for g in range(2):
            upper[pl.ds(2 * s + g, 1), :] = value[:, g * KP : g * KP + COEF]
    for n in range(3):
        upper[pl.ds(2 * NS + n, 1), :] = total[:, n * KP : n * KP + COEF]

    sent(rows)


def write_out(*refs):
    copies = [pltpu.make_async_copy(refs[n], refs[n + 3], refs[6].at[n]) for n in range(3)]
    for copy in copies:
        copy.start()
    for copy in copies:
        copy.wait()


def per_device(
    velocity, diffusion, advection, normals, tile_cell, tile_class, tile_leaf, tile_owner,
    source_expansion, translation, leaf_octant, node_octant, subtree_octant, cluster_octant, root_octant,
):
    vmem = pl.BlockSpec(memory_space=pltpu.VMEM)
    hbm = pl.BlockSpec(memory_space=pltpu.HBM)
    dma = pltpu.SemaphoreType.DMA
    rows = (SX + 2) * SLAB
    shapes = ((3, SX * SD, SPAN), (LEAVES, COEF), (2 * NS + 3, COEF))
    results = pl.pallas_call(
        kernel,
        out_shape=tuple(pltpu.VMEM(shape, F32) for shape in shapes),
        in_specs=[hbm] * 15,
        out_specs=(vmem, vmem, vmem),
        scratch_shapes=[
            pltpu.SMEM((1, TILES), I32),
            pltpu.SMEM((8, 8), I32),
            pltpu.SMEM((1, 8), I32),
            pltpu.SMEM((2, 8), I32),
            pltpu.SMEM((2, 8), I32),
            pltpu.SMEM((1, 8), I32),
            pltpu.VMEM((1, TILES), I32),
            pltpu.VMEM((1, TILES), I32),
            pltpu.VMEM((1, TILES), I32),
            pltpu.VMEM((3, SX, SD, SPAN), BF16),
            pltpu.VMEM((SX, SD, SPAN), BF16),
            pltpu.VMEM((SX, SD, SPAN), BF16),
            pltpu.VMEM((3, TILES, SPAN), BF16),
            pltpu.VMEM((8 * COEF, SPAN), BF16),
            pltpu.VMEM((8 * COEF, COEF - 2 * SPAN), F32),
            pltpu.VMEM((3, 8 * KR, SPAN), F32),
            pltpu.VMEM((8 * KP, SPAN), F32),
            pltpu.VMEM((8 * SPAN, KP), BF16),
            pltpu.VMEM((8, KP, 2 * KP), BF16),
            pltpu.VMEM((3, rows, SPAN), F32),
            pltpu.VMEM((3, rows, SPAN), F32),
            pltpu.VMEM((SX * SD, SPAN), F32),
            pltpu.VMEM((SX * SD, SPAN), F32),
            pltpu.VMEM((SX * SD, SPAN), F32),
            pltpu.VMEM((SLOTS, TILES), BF16),
            pltpu.VMEM((SLOTS, SLOTS), BF16),
            pltpu.VMEM((8 * LEAVES, SLOTS), BF16),
            pltpu.VMEM((3, TILES, SPAN), F32),
            pltpu.VMEM((SPAN, SPAN), BF16),
            pltpu.VMEM((SPAN, SPAN), BF16),
            pltpu.VMEM((KP, 6 * KP), BF16),
            pltpu.VMEM((SWEEPS, 2, 3, SD, SPAN), BF16),
            pltpu.VMEM((SWEEPS, 2, 3, SD, SPAN), BF16),
            pltpu.VMEM((SWEEPS, 2, 3, SX, SPAN), BF16),
            pltpu.VMEM((SWEEPS, 2, 3, SX, SPAN), BF16),
            pltpu.VMEM((ND, 2 * NS, SPAN), BF16),
            pltpu.VMEM((ND, 2 * NS, SPAN), BF16),
            pltpu.VMEM((NS, 2 * ND, SPAN), BF16),
            pltpu.VMEM((NS, 2 * ND, SPAN), BF16),
            pltpu.VMEM((ND, 2 * NS, SPAN), BF16),
            pltpu.VMEM((ND, 2 * NS, SPAN), BF16),
            pltpu.VMEM((NS, 2 * ND, SPAN), BF16),
            pltpu.VMEM((NS, 2 * ND, SPAN), BF16),
            pltpu.VMEM((1, 3 * KP), F32),
            pltpu.VMEM((ND, 1, 3 * KP), F32),
            pltpu.VMEM((1, 5 * KP), F32),
            pltpu.VMEM((NS, 1, 5 * KP), F32),
            dma((3, PARTS)),
            dma((14,)),
            dma((SWEEPS, 4, 3)),
            dma((SWEEPS, 4, 3)),
            dma((ND,)), dma((ND,)), dma((NS,)), dma((NS,)),
            dma((ND,)), dma((ND,)), dma((NS,)), dma((NS,)),
            dma((ND,)), dma((ND,)), dma((NS,)), dma((NS,)),
        ],
        compiler_params=pltpu.CompilerParams(
            collective_id=0, has_side_effects=True, vmem_limit_bytes=60400 * 1024
        ),
        cost_estimate=pl.CostEstimate(flops=10**8, bytes_accessed=12 * 10**6, transcendentals=0),
    )(
        tile_cell.reshape(1, TILES),
        leaf_octant.reshape(8, 8),
        node_octant.reshape(1, 8),
        subtree_octant.reshape(2, 8),
        cluster_octant,
        root_octant.reshape(1, 8),
        tile_owner.reshape(1, TILES),
        tile_class.reshape(1, TILES),
        tile_leaf.reshape(1, TILES),
        velocity,
        diffusion,
        advection,
        normals.reshape(3, TILES, SPAN),
        jnp.transpose(source_expansion, (2, 0, 1)).reshape(8 * COEF, SPAN),
        jnp.transpose(translation, (1, 0, 2)).reshape(8 * COEF, COEF),
    )
    flow, leaves, upper = pl.pallas_call(
        write_out,
        out_shape=tuple(jax.ShapeDtypeStruct(shape, F32) for shape in shapes),
        in_specs=[vmem] * 3,
        out_specs=[hbm] * 3,
        scratch_shapes=[dma((3,))],
        compiler_params=pltpu.CompilerParams(vmem_limit_bytes=1024 * 1024),
    )(*results)
    return flow.reshape(3, SX, SD, SPAN), leaves.reshape(1, 1, LEAVES, COEF), upper


def solution(mesh):
    in_specs = (
        P(None, "stream", "depth", None),
        P("stream", "depth", None),
        P("stream", "depth", None),
        P("stream", "depth", None, None, None),
        P("stream", "depth", None),
        P("stream", "depth", None),
        P("stream", "depth", None),
        P("stream", "depth", None, None),
        P(),
        P(),
        P("stream", "depth", None, None),
        P("stream", "depth", None),
        P("stream", None, None),
        P(),
        P(),
    )
    out_specs = (P(None, "stream", "depth", None), P("stream", "depth", None, None), P())
    return jax.shard_map(
        per_device, mesh=mesh, in_specs=in_specs, out_specs=out_specs, check_vma=False
    )
```
